512 devices in a mesh: dp: 64 (over z, x_hi, core), blk: 8 (over x_lo, y).
Axes of the slice: x: 4 (x_hi: 2, x_lo: 2; x = x_hi * 2 + x_lo), y: 4, z: 16, core: 2. Of those that a mesh axis runs over, the one named last changes fastest.
Arguments:
- tokens: bfloat16 [32768, 8192], P('dp', 'blk'), may hold values from -6 to 6
- up_right: bfloat16 [64, 128, 128], P('blk'), may hold values from -0.5 to 0.5
- up_left: bfloat16 [64, 128, 512], P('blk'), may hold values from -0.5 to 0.5
- down_right: bfloat16 [64, 512, 128], P('blk'), may hold values from -0.25 to 0.25
- down_left: bfloat16 [64, 128, 128], P('blk'), may hold values from -0.5 to 0.5
- cotangent: bfloat16 [32768, 8192], P('dp', 'blk'), may hold values from -6 to 6
Outputs:
- layer_out: bfloat16 [32768, 8192], P('dp', 'blk')
- input_grad: bfloat16 [32768, 8192], P('dp', 'blk')
- up_left_grad: float32 [64, 128, 512], P('blk', 'dp')
- down_left_grad: float32 [64, 128, 128], P('blk', 'dp')
The draws below stay inside these ranges and needn't reach their ends.
All inputs are finite; a program needn't handle non-finite values.
Results may differ from the reference program's by a relative error of at most 0.0068.
Values may be sent and summed in bfloat16 or wider, within the bound.
No kernel may reach another device: no remote copies, remote signals or barrier semaphores. Data moves between devices by JAX's collectives and lax.ppermute only.
A program may use at most 64 MiB of HBM per device.

```python
import math
import jax
import jax.numpy as jnp
from jax import lax

D = 8192
NBLK = 64
BIN = 128
BHID = 512
MIX = 2
TOKENS = 32768


def level_of(own_key, shape, cuts, least, high):
    loudness, own = 1.0, jax.random.fold_in(own_key, 6)
    for position, shards_of in cuts:
        heights = jnp.exp(jax.random.uniform(jax.random.fold_in(own, position), (shards_of,), jnp.float32, least / len(cuts), high / len(cuts)))
        loudness = loudness * jnp.repeat(heights, shape[position] // shards_of).reshape([-1 if axis == position else 1 for axis in range(len(shape))])
    return loudness


def gaussian(own_key, shape, spread, bound, shards=(), held_as=jnp.bfloat16):
    entries = jax.random.normal(own_key, shape, jnp.float32) * spread
    if len(shards) > 0:
        entries = level_of(own_key, shape, shards, -0.22, 0.18) * entries
    return jnp.clip(entries, min=-bound, max=bound).astype(held_as)


def setup_inputs(seed: int = 0) -> dict:
    keys = jax.random.split(jax.random.key(seed), 7)
    return {
        "tokens": gaussian(keys[0], (TOKENS, D), 1.0, 6.0, ((0, 64), (1, 8))),
        "up_right": gaussian(keys[1], (NBLK, BIN, BIN), BIN ** -0.5, 0.5, ((0, 8),)),
        "up_left": gaussian(keys[2], (NBLK, BIN, BHID), BIN ** -0.5, 0.5, ((0, 8),)),
        "down_right": gaussian(keys[3], (NBLK, BHID, BIN), BHID ** -0.5, 0.25, ((0, 8),)),
        "down_left": gaussian(keys[4], (NBLK, BIN, BIN), BIN ** -0.5, 0.5, ((0, 8),)),
        "cotangent": gaussian(keys[5], (TOKENS, D), 1.0, 6.0, ((0, 64), (1, 8))),
    }


def transpose_mix(blocks):
    count = blocks.shape[0]
    split = blocks.reshape(count, NBLK, NBLK, MIX)
    return split.transpose(0, 2, 1, 3).reshape(count, NBLK, BIN)

def reference(tokens, up_right, up_left, down_right, down_left, cotangent):
    bf16 = jnp.bfloat16
    f32 = jnp.float32
    block = math.gcd(TOKENS, 1024)
    count = TOKENS // block
    right_up = up_right.astype(f32)
    left_up = up_left.astype(f32)
    right_down = down_right.astype(f32)
    left_down = down_left.astype(f32)

    def advance(carry, pieces):
        up_total, down_total = carry
        inputs, backward = pieces
        split_in = inputs.reshape(block, NBLK, BIN).astype(f32)
        first = jnp.einsum('tki,kio->tko', split_in, right_up).astype(bf16)
        mixed = transpose_mix(first)
        before = jnp.einsum('tjc,jch->tjh', mixed.astype(f32), left_up)
        hidden = jax.nn.gelu(before).astype(bf16)
        second = jnp.einsum('tjh,jho->tjo', hidden.astype(f32), right_down).astype(bf16)
        mixed_down = transpose_mix(second)
        result = jnp.einsum('tkc,kco->tko', mixed_down.astype(f32), left_down).astype(bf16)
        upstream = backward.reshape(block, NBLK, BIN).astype(f32)
        grad_w = jnp.einsum('tko,kco->tkc', upstream, left_down).astype(bf16)
        down_total = down_total + jnp.einsum('tkc,tko->kco', mixed_down.astype(f32), upstream)
        grad_z = transpose_mix(grad_w)
        grad_hidden = jnp.einsum('tjo,jho->tjh', grad_z.astype(f32), right_down)
        unused, gelu_back = jax.vjp(jax.nn.gelu, before)
        grad_pre = gelu_back(grad_hidden)[0].astype(bf16)
        up_total = up_total + jnp.einsum('tjc,tjh->jch', mixed.astype(f32), grad_pre.astype(f32))
        grad_v = jnp.einsum('tjh,jch->tjc', grad_pre.astype(f32), left_up).astype(bf16)
        grad_u = transpose_mix(grad_v)
        grad_in = jnp.einsum('tko,kio->tki', grad_u.astype(f32), right_up).astype(bf16)
        return ((up_total, down_total), (result.reshape(block, D), grad_in.reshape(block, D)))
    start = (jnp.zeros((NBLK, BIN, BHID), f32), jnp.zeros((NBLK, BIN, BIN), f32))
    pieces = (tokens.reshape(count, block, D), cotangent.reshape(count, block, D))
    totals, outputs = lax.scan(advance, start, pieces)
    factor = 1.0 / math.sqrt(TOKENS)
    layer_out = outputs[0].reshape(TOKENS, D)
    input_grad = outputs[1].reshape(TOKENS, D)
    return (layer_out, input_grad, totals[0] * factor, totals[1] * factor)
```

```python
import functools
import math

import jax
import jax.numpy as jnp
from jax import lax
from jax.experimental import pallas as pl
from jax.experimental.pallas import tpu as pltpu
from jax.sharding import PartitionSpec as P

GROUPS = 8
OWNED = 8
BIN = 128
BHID = 512
ROWS = 512
PIECE = 16
MIB = 1 << 20
BF16 = jnp.bfloat16
F32 = jnp.float32

NN = (((1,), (0,)), ((), ()))
NT = (((1,), (1,)), ((), ()))
TN = (((0,), (0,)), ((), ()))
TT = (((0,), (1,)), ((), ()))


def dot(a, b, dims):
    return lax.dot_general(a, b, dims, preferred_element_type=F32)


def swap_matrix():
    to = lax.broadcasted_iota(jnp.int32, (BIN, BIN), 0)
    come = lax.broadcasted_iota(jnp.int32, (BIN, BIN), 1)
    wanted = ((to & 14) << 3) | ((to >> 4) << 1) | (to & 1)
    return jnp.where(come == wanted, 1.0, 0.0).astype(BF16)


def shard_matrix(core, xhi):
    to = lax.broadcasted_iota(jnp.int32, (BIN, BIN), 0)
    come = lax.broadcasted_iota(jnp.int32, (BIN, BIN), 1)
    of_core = (1 - (to >> 6)) ^ core
    of_xhi = (1 - ((to >> 5) & 1)) ^ xhi
    wanted = (((to >> 1) & 15) << 3) | (of_xhi << 2) | (of_core << 1) | (to & 1)
    return jnp.where(come == wanted, 1.0, 0.0).astype(BF16)


def scatter_rows(out_ref, block, value):
    at = pl.multiple_of(block * PIECE, PIECE)
    for n in range(GROUPS):
        out_ref[n, pl.ds(at, PIECE), :] = value[n * PIECE : (n + 1) * PIECE, :]


def gather_rows(msg_ref, held_ref):
    swap = swap_matrix()
    for src in range(GROUPS):
        swapped = dot(swap, msg_ref[src], NN).astype(BF16)
        for b in range(OWNED):
            held_ref[b, src * PIECE : (src + 1) * PIECE, :] = swapped[b * PIECE : (b + 1) * PIECE, :]


def right_kernel(dims, x_ref, w_ref, out_ref):
    for k in range(OWNED):
        value = dot(w_ref[k], x_ref[:, k * BIN : (k + 1) * BIN], dims).astype(BF16)
        scatter_rows(out_ref, k, value)


def up_kernel(place_ref, msg_ref, left_ref, down_ref, out_ref, saved_ref, slope_ref, held_ref, shard_ref):
    j = pl.program_id(0)

    @pl.when(j == 0)
    def _():
        gather_rows(msg_ref, held_ref)
        shard_ref[...] = shard_matrix(place_ref[0], place_ref[1])

    v = held_ref[j]
    saved_ref[0] = dot(shard_ref[...], v, NN).astype(BF16)
    s = dot(left_ref[0], v, TN)
    c = math.sqrt(2.0 / math.pi)
    square = s * s
    th = jnp.tanh(s * (c + (c * 0.044715) * square))
    half = 0.5 + 0.5 * th
    hidden = (s * half).astype(BF16)
    slope = half + (0.5 * s) * ((1.0 - th * th) * (c + (3.0 * c * 0.044715) * square))
    slope_ref[0] = slope.astype(BF16)
    z = dot(down_ref[0], hidden, TN).astype(BF16)
    scatter_rows(out_ref, j, z)


def back_kernel(msg_ref, saved_ref, slope_ref, left_ref, down_ref, out_ref, send_ref, keep_ref, held_ref):
    j = pl.program_id(0)

    @pl.when(j == 0)
    def _():
        gather_rows(msg_ref, held_ref)

    grad_hidden = dot(down_ref[0], held_ref[j], NN)
    grad_pre = (grad_hidden * slope_ref[0].astype(F32)).astype(BF16)
    grad_v = dot(left_ref[0], grad_pre, NN).astype(BF16)
    scatter_rows(out_ref, j, grad_v)
    part = dot(saved_ref[0], grad_pre, NT)
    send_ref[...] = part[: BIN // 2].astype(BF16)
    keep_ref[...] = part[BIN // 2 :]


def out_kernel(place_ref, msg_ref, left_ref, cot_ref, out_ref, send_ref, keep_ref, held_ref):
    gather_rows(msg_ref, held_ref)
    shard = shard_matrix(place_ref[0], place_ref[1])
    for k in range(OWNED):
        cols = slice(k * BIN, (k + 1) * BIN)
        w = held_ref[k]
        part = dot(dot(shard, w, NN).astype(BF16), cot_ref[:, cols], NN)
        send_ref[:, cols] = part[: BIN // 2].astype(BF16)
        keep_ref[:, cols] = part[BIN // 2 :]
        out_ref[:, cols] = dot(w, left_ref[k], TN).astype(BF16)


def in_kernel(msg_ref, right_ref, out_ref, held_ref):
    gather_rows(msg_ref, held_ref)
    for k in range(OWNED):
        out_ref[:, k * BIN : (k + 1) * BIN] = dot(held_ref[k], right_ref[k], TT).astype(BF16)


VMEM = pl.BlockSpec(memory_space=pltpu.VMEM)
SMEM = pl.BlockSpec(memory_space=pltpu.SMEM)
MSG = (GROUPS, BIN, ROWS)


def params():
    return pltpu.CompilerParams(vmem_limit_bytes=40 * MIB)


def cost(mflop, mib, trans=0):
    return pl.CostEstimate(flops=mflop * 1000000, bytes_accessed=mib * MIB, transcendentals=trans)


def shape(dims, dtype):
    return jax.ShapeDtypeStruct(dims, dtype)


def right(x, w, dims):
    return pl.pallas_call(
        functools.partial(right_kernel, dims),
        out_shape=shape(MSG, BF16),
        in_specs=[VMEM, VMEM],
        out_specs=VMEM,
        compiler_params=params(),
        cost_estimate=cost(134, 3),
    )(x, w)


def whole(dims):
    return pl.BlockSpec(dims, lambda j: (0,) * len(dims))


def each(dims):
    return pl.BlockSpec((1,) + dims, lambda j: (j, 0, 0))


def up(place, msg, left, down):
    return pl.pallas_call(
        up_kernel,
        grid=(OWNED,),
        out_shape=[shape(MSG, BF16), shape((OWNED, BIN, ROWS), BF16), shape((OWNED, BHID, ROWS), BF16)],
        in_specs=[SMEM, whole(MSG), each((BIN, BHID)), each((BHID, BIN))],
        out_specs=[whole(MSG), each((BIN, ROWS)), each((BHID, ROWS))],
        scratch_shapes=[pltpu.VMEM((OWNED, BIN, ROWS), BF16), pltpu.VMEM((BIN, BIN), BF16)],
        compiler_params=params(),
        cost_estimate=cost(1300, 9, OWNED * BHID * ROWS),
    )(place, msg, left, down)


def back(msg, saved, slope, left, down):
    half = (BIN // 2, OWNED * BHID)
    flat = pl.BlockSpec((BIN // 2, BHID), lambda j: (0, j))
    return pl.pallas_call(
        back_kernel,
        grid=(OWNED,),
        out_shape=[shape(MSG, BF16), shape(half, BF16), shape(half, F32)],
        in_specs=[whole(MSG), each((BIN, ROWS)), each((BHID, ROWS)), each((BIN, BHID)), each((BHID, BIN))],
        out_specs=[whole(MSG), flat, flat],
        scratch_shapes=[pltpu.VMEM((OWNED, BIN, ROWS), BF16)],
        compiler_params=params(),
        cost_estimate=cost(1800, 11),
    )(msg, saved, slope, left, down)


def out(place, msg, left, cot):
    half = (BIN // 2, OWNED * BIN)
    return pl.pallas_call(
        out_kernel,
        out_shape=[shape((ROWS, OWNED * BIN), BF16), shape(half, BF16), shape(half, F32)],
        in_specs=[SMEM, VMEM, VMEM, VMEM],
        out_specs=[VMEM, VMEM, VMEM],
        scratch_shapes=[pltpu.VMEM((OWNED, BIN, ROWS), BF16)],
        compiler_params=params(),
        cost_estimate=cost(500, 4),
    )(place, msg, left, cot)


def into(msg, rightw):
    return pl.pallas_call(
        in_kernel,
        out_shape=shape((ROWS, OWNED * BIN), BF16),
        in_specs=[VMEM, VMEM],
        out_specs=VMEM,
        scratch_shapes=[pltpu.VMEM((OWNED, BIN, ROWS), BF16)],
        compiler_params=params(),
        cost_estimate=cost(300, 3),
    )(msg, rightw)


def exchange(msg):
    return lax.all_to_all(msg, "blk", split_axis=0, concat_axis=0, tiled=True)


def sum_over_dp(send, keep, width, factor):
    count = lax.axis_size("dp")
    depth = count // 4
    rows = keep.shape[0] // 2
    total = keep + lax.ppermute(send, "dp", [(d, d ^ 1) for d in range(count)]).astype(F32)
    far = lax.ppermute(total[:rows].astype(BF16), "dp", [(d, d ^ 2) for d in range(count)])
    total = (total[rows:] + far.astype(F32)).astype(BF16)
    lanes = [[z * 4 + low for z in range(depth)] for low in range(4)]
    pieces = lax.all_to_all(
        total.reshape(depth, rows // depth, -1), "dp", 0, 0, axis_index_groups=lanes, tiled=True
    )
    summed = jnp.sum(pieces.astype(F32), axis=0) * factor
    return summed.reshape(rows // depth, OWNED, width).transpose(1, 0, 2)


def on_device(tokens, up_right, up_left, down_right, down_left, cotangent):
    at = lax.axis_index("dp")
    place = jnp.stack([at & 1, (at >> 1) & 1]).astype(jnp.int32)
    factor = 1.0 / math.sqrt(tokens.shape[0] * lax.axis_size("dp"))
    v = exchange(right(tokens, up_right, TT))
    grad_z = exchange(right(cotangent, down_left, NT))
    z, saved, slope = up(place, v, up_left, down_right)
    w = exchange(z)
    grad_v, up_send, up_keep = back(grad_z, saved, slope, up_left, down_right)
    grad_u = exchange(grad_v)
    up_grad = sum_over_dp(up_send, up_keep, BHID, factor)
    layer_out, down_send, down_keep = out(place, w, down_left, cotangent)
    down_grad = sum_over_dp(down_send, down_keep, BIN, factor)
    input_grad = into(grad_u, up_right)
    return (layer_out, input_grad, up_grad, down_grad)


def solution(mesh):
    placed = (
        P("dp", "blk"),
        P("blk", None, None),
        P("blk", None, None),
        P("blk", None, None),
        P("blk", None, None),
        P("dp", "blk"),
    )
    return jax.shard_map(
        on_device,
        mesh=mesh,
        in_specs=placed,
        out_specs=(P("dp", "blk"), P("dp", "blk"), P("blk", "dp", None), P("blk", "dp", None)),
        check_vma=False,
    )
```

```python
import functools
import math

import jax
import jax.numpy as jnp
from jax import lax
from jax.experimental import pallas as pl
from jax.experimental.pallas import tpu as pltpu
from jax.sharding import PartitionSpec as P

GROUPS = 8
OWNED = 8
BIN = 128
BHID = 512
ROWS = 512
PIECE = 16
PAIR = 2
STEPS = (0, 2, 3, 1, 4, 5)
MIB = 1 << 20
BF16 = jnp.bfloat16
F32 = jnp.float32

NN = (((1,), (0,)), ((), ()))
NT = (((1,), (1,)), ((), ()))
TN = (((0,), (0,)), ((), ()))
TT = (((0,), (1,)), ((), ()))


def dot(a, b, dims):
    return lax.dot_general(a, b, dims, preferred_element_type=F32)


def swap_matrix():
    to = lax.broadcasted_iota(jnp.int32, (BIN, BIN), 0)
    come = lax.broadcasted_iota(jnp.int32, (BIN, BIN), 1)
    wanted = ((to & 14) << 3) | ((to >> 4) << 1) | (to & 1)
    return jnp.where(come == wanted, 1.0, 0.0).astype(BF16)


def shard_matrix(place):
    to = lax.broadcasted_iota(jnp.int32, (BIN, BIN), 0)
    come = lax.broadcasted_iota(jnp.int32, (BIN, BIN), 1)
    theirs = jnp.zeros_like(to)
    for step, bit in enumerate(STEPS):
        theirs = theirs | ((1 - ((to >> (len(STEPS) - step)) & 1)) << bit)
    wanted = ((theirs ^ place) << 1) | (to & 1)
    return jnp.where(come == wanted, 1.0, 0.0).astype(BF16)


def scatter_rows(out_ref, slot, value):
    for n in range(GROUPS):
        out_ref[n, slot * PIECE : (slot + 1) * PIECE, :] = value[n * PIECE : (n + 1) * PIECE, :]


def gather_rows(msg_ref, held_ref):
    swap = swap_matrix()
    for src in range(GROUPS):
        swapped = dot(swap, msg_ref[src], NN).astype(BF16)
        for b in range(OWNED):
            held_ref[b, src * PIECE : (src + 1) * PIECE, :] = swapped[b * PIECE : (b + 1) * PIECE, :]


def right_kernel(dims, x_ref, w_ref, out_ref):
    for k in range(PAIR):
        value = dot(w_ref[k], x_ref[:, k * BIN : (k + 1) * BIN], dims).astype(BF16)
        scatter_rows(out_ref, k, value)


def up_kernel(place_ref, msg_ref, left_ref, down_ref, out_ref, saved_ref, slope_ref, held_ref, shard_ref):
    j = pl.program_id(0)

    @pl.when(j == 0)
    def _():
        gather_rows(msg_ref, held_ref)
        shard_ref[...] = shard_matrix(place_ref[0])

    v = held_ref[j]
    saved_ref[0] = dot(shard_ref[...], v, NN).astype(BF16)
    s = dot(left_ref[0], v, TN)
    c = math.sqrt(2.0 / math.pi)
    square = s * s
    th = jnp.tanh(s * (c + (c * 0.044715) * square))
    half = 0.5 + 0.5 * th
    hidden = (s * half).astype(BF16)
    slope = half + (0.5 * s) * ((1.0 - th * th) * (c + (3.0 * c * 0.044715) * square))
    slope_ref[0] = slope.astype(BF16)
    z = dot(down_ref[0], hidden, TN).astype(BF16)
    scatter_rows(out_ref, 0, z)


def back_kernel(msg_ref, saved_ref, slope_ref, left_ref, down_ref, out_ref, send_ref, keep_ref, held_ref):
    j = pl.program_id(0)

    @pl.when(j == 0)
    def _():
        gather_rows(msg_ref, held_ref)

    grad_hidden = dot(down_ref[0], held_ref[j], NN)
    grad_pre = (grad_hidden * slope_ref[0].astype(F32)).astype(BF16)
    grad_v = dot(left_ref[0], grad_pre, NN).astype(BF16)
    scatter_rows(out_ref, 0, grad_v)
    part = dot(saved_ref[0], grad_pre, NT)
    send_ref[...] = part[: BIN // 2].astype(BF16)
    keep_ref[...] = part[BIN // 2 :]


def out_kernel(place_ref, msg_ref, left_ref, cot_ref, out_ref, send_ref, keep_ref, held_ref, shard_ref):
    step = pl.program_id(0)

    @pl.when(step == 0)
    def _():
        gather_rows(msg_ref, held_ref)
        shard_ref[...] = shard_matrix(place_ref[0])

    for k in range(PAIR):
        cols = slice(k * BIN, (k + 1) * BIN)
        w = held_ref[step * PAIR + k]
        part = dot(dot(shard_ref[...], w, NN).astype(BF16), cot_ref[:, cols], NN)
        send_ref[:, cols] = part[: BIN // 2].astype(BF16)
        keep_ref[:, cols] = part[BIN // 2 :]
        out_ref[:, cols] = dot(w, left_ref[k], TN).astype(BF16)


def in_kernel(msg_ref, right_ref, out_ref, held_ref):
    step = pl.program_id(0)

    @pl.when(step == 0)
    def _():
        gather_rows(msg_ref, held_ref)

    for k in range(PAIR):
        w = held_ref[step * PAIR + k]
        out_ref[:, k * BIN : (k + 1) * BIN] = dot(w, right_ref[k], TT).astype(BF16)


VMEM = pl.BlockSpec(memory_space=pltpu.VMEM)
SMEM = pl.BlockSpec(memory_space=pltpu.SMEM)
MSG = (GROUPS, BIN, ROWS)


def params(mib):
    return pltpu.CompilerParams(vmem_limit_bytes=mib * MIB)


def cost(mflop, mib, trans=0):
    return pl.CostEstimate(flops=mflop * 1000000, bytes_accessed=mib * MIB, transcendentals=trans)


def shape(dims, dtype):
    return jax.ShapeDtypeStruct(dims, dtype)


def far(dims, dtype):
    return pltpu.HBM(dims, dtype)


def stay(x):
    return pltpu.with_memory_space_constraint(x, pltpu.HBM)


def each(dims, count=1):
    return pl.BlockSpec((count,) + dims, lambda j: (j, 0, 0))


def pieces(count):
    return pl.BlockSpec((GROUPS, count * PIECE, ROWS), lambda j: (0, j, 0))


def columns(rows, width):
    return pl.BlockSpec((rows, width), lambda j: (0, j))


HELD = pltpu.VMEM((OWNED, BIN, ROWS), BF16)
SHARD = pltpu.VMEM((BIN, BIN), BF16)


def right(x, w, dims):
    return pl.pallas_call(
        functools.partial(right_kernel, dims),
        grid=(OWNED // PAIR,),
        out_shape=far(MSG, BF16),
        in_specs=[columns(ROWS, PAIR * BIN), each((BIN, BIN), PAIR)],
        out_specs=pieces(PAIR),
        compiler_params=params(16),
        cost_estimate=cost(134, 3),
    )(stay(x), stay(w))


def up(place, msg, left, down):
    return pl.pallas_call(
        up_kernel,
        grid=(OWNED,),
        out_shape=[far(MSG, BF16), far((OWNED, BIN, ROWS), BF16), far((OWNED, BHID, ROWS), BF16)],
        in_specs=[SMEM, VMEM, each((BIN, BHID)), each((BHID, BIN))],
        out_specs=[pieces(1), each((BIN, ROWS)), each((BHID, ROWS))],
        scratch_shapes=[HELD, SHARD],
        compiler_params=params(24),
        cost_estimate=cost(1300, 9, OWNED * BHID * ROWS),
    )(place, msg, stay(left), stay(down))


def back(msg, saved, slope, left, down):
    half = (BIN // 2, OWNED * BHID)
    return pl.pallas_call(
        back_kernel,
        grid=(OWNED,),
        out_shape=[far(MSG, BF16), far(half, BF16), far(half, F32)],
        in_specs=[VMEM, each((BIN, ROWS)), each((BHID, ROWS)), each((BIN, BHID)), each((BHID, BIN))],
        out_specs=[pieces(1), columns(BIN // 2, BHID), columns(BIN // 2, BHID)],
        scratch_shapes=[HELD],
        compiler_params=params(24),
        cost_estimate=cost(1800, 11),
    )(msg, stay(saved), stay(slope), stay(left), stay(down))


def out(place, msg, left, cot):
    half = (BIN // 2, OWNED * BIN)
    wide = PAIR * BIN
    return pl.pallas_call(
        out_kernel,
        grid=(OWNED // PAIR,),
        out_shape=[far((ROWS, OWNED * BIN), BF16), shape(half, BF16), shape(half, F32)],
        in_specs=[SMEM, VMEM, each((BIN, BIN), PAIR), columns(ROWS, wide)],
        out_specs=[columns(ROWS, wide), columns(BIN // 2, wide), columns(BIN // 2, wide)],
        scratch_shapes=[HELD, SHARD],
        compiler_params=params(20),
        cost_estimate=cost(500, 4),
    )(place, msg, stay(left), stay(cot))


def into(msg, rightw):
    return pl.pallas_call(
        in_kernel,
        grid=(OWNED // PAIR,),
        out_shape=far((ROWS, OWNED * BIN), BF16),
        in_specs=[VMEM, each((BIN, BIN), PAIR)],
        out_specs=columns(ROWS, PAIR * BIN),
        scratch_shapes=[HELD],
        compiler_params=params(20),
        cost_estimate=cost(300, 3),
    )(msg, stay(rightw))


def exchange(msg):
    return lax.all_to_all(msg, "blk", split_axis=0, concat_axis=0, tiled=True)


def join_kernel(up_keep_ref, up_far_ref, down_keep_ref, down_far_ref, send_ref, keep_ref):
    half = send_ref.shape[0]
    at = 0
    for kept, far in ((up_keep_ref, up_far_ref), (down_keep_ref, down_far_ref)):
        cols = slice(at, at + kept.shape[1])
        at += kept.shape[1]
        total = kept[...] + far[...].astype(F32)
        send_ref[:, cols] = total[:half].astype(BF16)
        keep_ref[:, cols] = total[half:]


def join(up_keep, up_far, down_keep, down_far):
    dims = (up_keep.shape[0] // 2, up_keep.shape[1] + down_keep.shape[1])
    return pl.pallas_call(
        join_kernel,
        out_shape=[shape(dims, BF16), shape(dims, F32)],
        in_specs=[VMEM] * 4,
        out_specs=[VMEM] * 2,
        compiler_params=params(8),
        cost_estimate=cost(1, 3),
    )(up_keep, up_far, down_keep, down_far)


def swap_halves(send, step):
    bit = 1 << STEPS[step]
    return lax.ppermute(send, "dp", [(d, d ^ bit) for d in range(lax.axis_size("dp"))])


def halve(send, keep, step):
    total = keep + swap_halves(send, step).astype(F32)
    rows = total.shape[0] // 2
    return total[:rows].astype(BF16), total[rows:]


def sum_over_dp(up_send, up_keep, down_send, down_keep, grad_u, factor):
    for step in range(2):
        up_send, up_keep = halve(up_send, up_keep, step)
        down_send, down_keep = halve(down_send, down_keep, step)
    up_far, down_far = swap_halves(up_send, 2), swap_halves(down_send, 2)
    send, keep = join(up_keep, up_far, down_keep, down_far)
    send, grad_u = lax.optimization_barrier((send, grad_u))
    for step in range(3, len(STEPS) - 1):
        send, keep = halve(send, keep, step)
    total = (keep + swap_halves(send, len(STEPS) - 1).astype(F32)) * factor
    split = OWNED * BHID
    up_grad = total[:, :split].reshape(-1, OWNED, BHID).transpose(1, 0, 2)
    down_grad = total[:, split:].reshape(-1, OWNED, BIN).transpose(1, 0, 2)
    return up_grad, down_grad, grad_u


def on_device(tokens, up_right, up_left, down_right, down_left, cotangent):
    place = lax.axis_index("dp").reshape(1).astype(jnp.int32)
    factor = 1.0 / math.sqrt(tokens.shape[0] * lax.axis_size("dp"))
    v = exchange(right(tokens, up_right, TT))
    grad_z = exchange(right(cotangent, down_left, NT))
    z, saved, slope = up(place, v, up_left, down_right)
    w = exchange(z)
    grad_v, up_send, up_keep = back(grad_z, saved, slope, up_left, down_right)
    grad_u = exchange(grad_v)
    layer_out, down_send, down_keep = out(place, w, down_left, cotangent)
    up_grad, down_grad, grad_u = sum_over_dp(
        up_send, up_keep, down_send, down_keep, grad_u, factor
    )
    input_grad = into(grad_u, up_right)
    return (layer_out, input_grad, up_grad, down_grad)


def solution(mesh):
    placed = (
        P("dp", "blk"),
        P("blk", None, None),
        P("blk", None, None),
        P("blk", None, None),
        P("blk", None, None),
        P("dp", "blk"),
    )
    return jax.shard_map(
        on_device,
        mesh=mesh,
        in_specs=placed,
        out_specs=(P("dp", "blk"), P("dp", "blk"), P("blk", "dp", None), P("blk", "dp", None)),
        check_vma=False,
    )
```

```python
import functools
import math

import jax
import jax.numpy as jnp
from jax import lax
from jax.experimental import pallas as pl
from jax.experimental.pallas import tpu as pltpu
from jax.sharding import PartitionSpec as P

GROUPS = 8
OWNED = 8
BIN = 128
BHID = 512
ROWS = 512
PIECE = 16
PAIR = 2
STEPS = (0, 2, 3)
SHARED = (5, 4, 1)
MIB = 1 << 20
BF16 = jnp.bfloat16
F32 = jnp.float32

NN = (((1,), (0,)), ((), ()))
NT = (((1,), (1,)), ((), ()))
TN = (((0,), (0,)), ((), ()))
TT = (((0,), (1,)), ((), ()))


def dot(a, b, dims):
    return lax.dot_general(a, b, dims, preferred_element_type=F32)


def swap_matrix():
    to = lax.broadcasted_iota(jnp.int32, (BIN, BIN), 0)
    come = lax.broadcasted_iota(jnp.int32, (BIN, BIN), 1)
    wanted = ((to & 14) << 3) | ((to >> 4) << 1) | (to & 1)
    return jnp.where(come == wanted, 1.0, 0.0).astype(BF16)


def shard_matrix(place):
    to = lax.broadcasted_iota(jnp.int32, (BIN, BIN), 0)
    come = lax.broadcasted_iota(jnp.int32, (BIN, BIN), 1)
    owner = jnp.zeros_like(to)
    for at, bit in enumerate(STEPS + SHARED):
        here = (to >> (len(STEPS + SHARED) - at)) & 1
        if bit in STEPS:
            here = (1 - here) ^ ((place >> bit) & 1)
        owner = owner | (here << bit)
    return jnp.where(come == ((owner << 1) | (to & 1)), 1.0, 0.0).astype(BF16)


def scatter_rows(out_ref, slot, value):
    for n in range(GROUPS):
        out_ref[n, slot * PIECE : (slot + 1) * PIECE, :] = value[n * PIECE : (n + 1) * PIECE, :]


def gather_rows(msg_ref, held_ref):
    swap = swap_matrix()
    for src in range(GROUPS):
        swapped = dot(swap, msg_ref[src], NN).astype(BF16)
        for b in range(OWNED):
            held_ref[b, src * PIECE : (src + 1) * PIECE, :] = swapped[b * PIECE : (b + 1) * PIECE, :]


def fetch(src, dst, sem):
    copy = pltpu.make_async_copy(src, dst, sem)
    copy.start()
    return copy


def right_kernel(dims, x_hbm, w_hbm, out_hbm, x_ref, w_ref, out_ref, w_sem, in_sem, out_sem):
    w_copy = fetch(w_hbm, w_ref, w_sem)
    wide = PAIR * BIN
    x_copies = []
    for p in range(OWNED // PAIR):
        cols = pl.ds(p * wide, wide)
        x_copies.append(fetch(x_hbm.at[:, cols], x_ref.at[:, cols], in_sem.at[p]))
    w_copy.wait()
    out_copies = []
    for p in range(OWNED // PAIR):
        x_copies[p].wait()
        for k in range(p * PAIR, (p + 1) * PAIR):
            value = dot(w_ref[k], x_ref[:, k * BIN : (k + 1) * BIN], dims).astype(BF16)
            scatter_rows(out_ref, k, value)
        rows = pl.ds(p * PAIR * PIECE, PAIR * PIECE)
        out_copies.append(fetch(out_ref.at[:, rows, :], out_hbm.at[:, rows, :], out_sem.at[p]))
    for copy in out_copies:
        copy.wait()


def up_kernel(place_ref, msg_ref, left_ref, down_ref, out_ref, saved_ref, slope_ref, held_ref, shard_ref):
    j = pl.program_id(0)

    @pl.when(j == 0)
    def _():
        gather_rows(msg_ref, held_ref)
        shard_ref[...] = shard_matrix(place_ref[0])

    v = held_ref[j]
    saved_ref[0] = dot(shard_ref[...], v, NN).astype(BF16)
    s = dot(left_ref[0], v, TN)
    c = math.sqrt(2.0 / math.pi)
    square = s * s
    th = jnp.tanh(s * (c + (c * 0.044715) * square))
    half = 0.5 + 0.5 * th
    hidden = (s * half).astype(BF16)
    slope = half + (0.5 * s) * ((1.0 - th * th) * (c + (3.0 * c * 0.044715) * square))
    slope_ref[0] = slope.astype(BF16)
    z = dot(down_ref[0], hidden, TN).astype(BF16)
    scatter_rows(out_ref, 0, z)


def back_kernel(msg_ref, saved_ref, slope_ref, left_ref, down_ref, out_ref, send_ref, keep_ref, held_ref):
    j = pl.program_id(0)

    @pl.when(j == 0)
    def _():
        gather_rows(msg_ref, held_ref)

    grad_hidden = dot(down_ref[0], held_ref[j], NN)
    grad_pre = (grad_hidden * slope_ref[0].astype(F32)).astype(BF16)
    grad_v = dot(left_ref[0], grad_pre, NN).astype(BF16)
    scatter_rows(out_ref, 0, grad_v)
    part = dot(saved_ref[0], grad_pre, NT)
    send_ref[...] = part[: BIN // 2].astype(BF16)
    keep_ref[...] = part[BIN // 2 :]


def out_kernel(
    place_ref, msg_ref, left_hbm, cot_hbm, out_hbm, send_ref, keep_ref,
    held_ref, left_ref, cot_ref, out_ref, left_sem, in_sem, out_sem,
):
    wide = PAIR * BIN
    left_copy = fetch(left_hbm, left_ref, left_sem)
    cot_copies = []
    for p in range(OWNED // PAIR):
        cols = pl.ds(p * wide, wide)
        cot_copies.append(fetch(cot_hbm.at[:, cols], cot_ref.at[:, cols], in_sem.at[p]))
    gather_rows(msg_ref, held_ref)
    shard = shard_matrix(place_ref[0])
    left_copy.wait()
    out_copies = []
    for p in range(OWNED // PAIR):
        cot_copies[p].wait()
        for k in range(p * PAIR, (p + 1) * PAIR):
            cols = slice(k * BIN, (k + 1) * BIN)
            w = held_ref[k]
            part = dot(dot(shard, w, NN).astype(BF16), cot_ref[:, cols], NN)
            send_ref[:, cols] = part[: BIN // 2].astype(BF16)
            keep_ref[:, cols] = part[BIN // 2 :]
            out_ref[:, cols] = dot(w, left_ref[k], TN).astype(BF16)
        cols = pl.ds(p * wide, wide)
        out_copies.append(fetch(out_ref.at[:, cols], out_hbm.at[:, cols], out_sem.at[p]))
    for copy in out_copies:
        copy.wait()


def in_kernel(msg_ref, right_hbm, out_hbm, held_ref, right_ref, out_ref, right_sem, out_sem):
    wide = PAIR * BIN
    right_copy = fetch(right_hbm, right_ref, right_sem)
    gather_rows(msg_ref, held_ref)
    right_copy.wait()
    out_copies = []
    for p in range(OWNED // PAIR):
        for k in range(p * PAIR, (p + 1) * PAIR):
            out_ref[:, k * BIN : (k + 1) * BIN] = dot(held_ref[k], right_ref[k], TT).astype(BF16)
        cols = pl.ds(p * wide, wide)
        out_copies.append(fetch(out_ref.at[:, cols], out_hbm.at[:, cols], out_sem.at[p]))
    for copy in out_copies:
        copy.wait()


VMEM = pl.BlockSpec(memory_space=pltpu.VMEM)
SMEM = pl.BlockSpec(memory_space=pltpu.SMEM)
MSG = (GROUPS, BIN, ROWS)


def params(mib):
    return pltpu.CompilerParams(vmem_limit_bytes=mib * MIB)


def cost(mflop, mib, trans=0):
    return pl.CostEstimate(flops=mflop * 1000000, bytes_accessed=mib * MIB, transcendentals=trans)


def shape(dims, dtype):
    return jax.ShapeDtypeStruct(dims, dtype)


def far(dims, dtype):
    return pltpu.HBM(dims, dtype)


def stay(x):
    return pltpu.with_memory_space_constraint(x, pltpu.HBM)


def each(dims, count=1):
    return pl.BlockSpec((count,) + dims, lambda j: (j, 0, 0))


def pieces(count):
    return pl.BlockSpec((GROUPS, count * PIECE, ROWS), lambda j: (0, j, 0))


def columns(rows, width):
    return pl.BlockSpec((rows, width), lambda j: (0, j))


HELD = pltpu.VMEM((OWNED, BIN, ROWS), BF16)
SHARD = pltpu.VMEM((BIN, BIN), BF16)


ANY = pl.BlockSpec(memory_space=pl.ANY)
SQUARES = pltpu.VMEM((OWNED, BIN, BIN), BF16)
FLAT = pltpu.VMEM((ROWS, OWNED * BIN), BF16)
ONE = pltpu.SemaphoreType.DMA
SEMS = pltpu.SemaphoreType.DMA((OWNED // PAIR,))


def right(x, w, dims):
    return pl.pallas_call(
        functools.partial(right_kernel, dims),
        out_shape=far(MSG, BF16),
        in_specs=[ANY, ANY],
        out_specs=ANY,
        scratch_shapes=[FLAT, SQUARES, pltpu.VMEM(MSG, BF16), ONE, SEMS, SEMS],
        compiler_params=params(16),
        cost_estimate=cost(134, 3),
    )(stay(x), stay(w))


def up(place, msg, left, down):
    return pl.pallas_call(
        up_kernel,
        grid=(OWNED,),
        out_shape=[far(MSG, BF16), far((OWNED, BIN, ROWS), BF16), far((OWNED, BHID, ROWS), BF16)],
        in_specs=[SMEM, VMEM, each((BIN, BHID)), each((BHID, BIN))],
        out_specs=[pieces(1), each((BIN, ROWS)), each((BHID, ROWS))],
        scratch_shapes=[HELD, SHARD],
        compiler_params=params(24),
        cost_estimate=cost(1300, 9, OWNED * BHID * ROWS),
    )(place, msg, stay(left), stay(down))


def back(msg, saved, slope, left, down):
    half = (BIN // 2, OWNED * BHID)
    return pl.pallas_call(
        back_kernel,
        grid=(OWNED,),
        out_shape=[far(MSG, BF16), far(half, BF16), far(half, F32)],
        in_specs=[VMEM, each((BIN, ROWS)), each((BHID, ROWS)), each((BIN, BHID)), each((BHID, BIN))],
        out_specs=[pieces(1), columns(BIN // 2, BHID), columns(BIN // 2, BHID)],
        scratch_shapes=[HELD],
        compiler_params=params(24),
        cost_estimate=cost(1800, 11),
    )(msg, stay(saved), stay(slope), stay(left), stay(down))


def out(place, msg, left, cot):
    half = (BIN // 2, OWNED * BIN)
    return pl.pallas_call(
        out_kernel,
        out_shape=[far((ROWS, OWNED * BIN), BF16), far(half, BF16), far(half, F32)],
        in_specs=[SMEM, VMEM, ANY, ANY],
        out_specs=[ANY, VMEM, VMEM],
        scratch_shapes=[HELD, SQUARES, FLAT, FLAT, ONE, SEMS, SEMS],
        compiler_params=params(20),
        cost_estimate=cost(3000, 16),
    )(place, msg, stay(left), stay(cot))


def into(msg, rightw):
    return pl.pallas_call(
        in_kernel,
        out_shape=far((ROWS, OWNED * BIN), BF16),
        in_specs=[VMEM, ANY],
        out_specs=ANY,
        scratch_shapes=[HELD, SQUARES, FLAT, ONE, SEMS],
        compiler_params=params(20),
        cost_estimate=cost(300, 3),
    )(msg, stay(rightw))


def exchange(msg):
    return lax.all_to_all(msg, "blk", split_axis=0, concat_axis=0, tiled=True)


def join_kernel(up_keep_ref, up_far_ref, down_keep_ref, down_far_ref, out_ref):
    at = 0
    for kept, far_ref in ((up_keep_ref, up_far_ref), (down_keep_ref, down_far_ref)):
        cols = slice(at, at + kept.shape[1])
        at += kept.shape[1]
        total = (kept[...] + far_ref[...].astype(F32)).astype(BF16)
        for n in range(out_ref.shape[0]):
            out_ref[n, :, cols] = total[2 * n : 2 * n + 2]


def join(up_keep, up_far, down_keep, down_far):
    dims = (up_keep.shape[0] // 2, 2, up_keep.shape[1] + down_keep.shape[1])
    return pl.pallas_call(
        join_kernel,
        out_shape=shape(dims, BF16),
        in_specs=[VMEM] * 4,
        out_specs=VMEM,
        compiler_params=params(8),
        cost_estimate=cost(1, 1),
    )(up_keep, up_far, down_keep, down_far)


def swap_halves(send, step):
    bit = 1 << STEPS[step]
    return lax.ppermute(send, "dp", [(d, d ^ bit) for d in range(lax.axis_size("dp"))])


def halve(send, keep, step):
    total = keep + swap_halves(send, step).astype(F32)
    rows = total.shape[0] // 2
    return total[:rows].astype(BF16), total[rows:]


def sum_over_dp(up_send, up_keep, down_send, down_keep, grad_u, factor):
    for step in range(len(STEPS) - 1):
        up_send, up_keep = halve(up_send, up_keep, step)
        down_send, down_keep = halve(down_send, down_keep, step)
    last = len(STEPS) - 1
    up_far, down_far = swap_halves(up_send, last), swap_halves(down_send, last)
    total = join(up_keep, up_far, down_keep, down_far)
    total, grad_u = lax.optimization_barrier((total, grad_u))
    count = lax.axis_size("dp")
    mask = sum(1 << bit for bit in SHARED)
    groups = []
    for first in range(count):
        if first & mask == 0:
            members = [0]
            for bit in SHARED:
                members = [m | (b << bit) for m in members for b in (0, 1)]
            groups.append([first | m for m in members])
    total = lax.all_to_all(total, "dp", 0, 0, axis_index_groups=groups, tiled=True)
    total = jnp.sum(total.astype(F32), axis=0) * factor
    split = OWNED * BHID
    up_grad = total[:, :split].reshape(-1, OWNED, BHID).transpose(1, 0, 2)
    down_grad = total[:, split:].reshape(-1, OWNED, BIN).transpose(1, 0, 2)
    return up_grad, down_grad, grad_u


def on_device(tokens, up_right, up_left, down_right, down_left, cotangent):
    place = lax.axis_index("dp").reshape(1).astype(jnp.int32)
    factor = 1.0 / math.sqrt(tokens.shape[0] * lax.axis_size("dp"))
    v = exchange(right(tokens, up_right, TT))
    grad_z = exchange(right(cotangent, down_left, NT))
    z, saved, slope = up(place, v, up_left, down_right)
    w = exchange(z)
    grad_v, up_send, up_keep = back(grad_z, saved, slope, up_left, down_right)
    grad_u = exchange(grad_v)
    layer_out, down_send, down_keep = out(place, w, down_left, cotangent)
    up_grad, down_grad, grad_u = sum_over_dp(
        up_send, up_keep, down_send, down_keep, grad_u, factor
    )
    input_grad = into(grad_u, up_right)
    return (layer_out, input_grad, up_grad, down_grad)


def solution(mesh):
    placed = (
        P("dp", "blk"),
        P("blk", None, None),
        P("blk", None, None),
        P("blk", None, None),
        P("blk", None, None),
        P("dp", "blk"),
    )
    return jax.shard_map(
        on_device,
        mesh=mesh,
        in_specs=placed,
        out_specs=(P("dp", "blk"), P("dp", "blk"), P("blk", "dp", None), P("blk", "dp", None)),
        check_vma=False,
    )
```

```python
import functools
import math

import jax
import jax.numpy as jnp
from jax import lax
from jax.experimental import pallas as pl
from jax.experimental.pallas import tpu as pltpu
from jax.sharding import PartitionSpec as P

GROUPS = 8
OWNED = 8
BIN = 128
BHID = 512
ROWS = 512
PIECE = 16
PAIR = 2
STEPS = (0, 2)
SHARED = (5, 4, 3, 1)
DP = ("z8", "z4", "z2", "z1", "far", "core")
MIB = 1 << 20
BF16 = jnp.bfloat16
F32 = jnp.float32

NN = (((1,), (0,)), ((), ()))
NT = (((1,), (1,)), ((), ()))
TN = (((0,), (0,)), ((), ()))
TT = (((0,), (1,)), ((), ()))


def dot(a, b, dims):
    return lax.dot_general(a, b, dims, preferred_element_type=F32)


def swap_matrix():
    to = lax.broadcasted_iota(jnp.int32, (BIN, BIN), 0)
    come = lax.broadcasted_iota(jnp.int32, (BIN, BIN), 1)
    wanted = ((to & 14) << 3) | ((to >> 4) << 1) | (to & 1)
    return jnp.where(come == wanted, 1.0, 0.0).astype(BF16)


def shard_matrix(place):
    to = lax.broadcasted_iota(jnp.int32, (BIN, BIN), 0)
    come = lax.broadcasted_iota(jnp.int32, (BIN, BIN), 1)
    owner = jnp.zeros_like(to)
    for at, bit in enumerate(STEPS + SHARED):
        here = (to >> (len(STEPS + SHARED) - at)) & 1
        if bit in STEPS:
            here = (1 - here) ^ ((place >> bit) & 1)
        owner = owner | (here << bit)
    return jnp.where(come == ((owner << 1) | (to & 1)), 1.0, 0.0).astype(BF16)


def scatter_rows(out_ref, slot, value):
    for n in range(GROUPS):
        out_ref[n, slot * PIECE : (slot + 1) * PIECE, :] = value[n * PIECE : (n + 1) * PIECE, :]


def gather_rows(msg_ref, held_ref):
    swap = swap_matrix()
    for src in range(GROUPS):
        swapped = dot(swap, msg_ref[src], NN).astype(BF16)
        for b in range(OWNED):
            held_ref[b, src * PIECE : (src + 1) * PIECE, :] = swapped[b * PIECE : (b + 1) * PIECE, :]


def fetch(src, dst, sem):
    copy = pltpu.make_async_copy(src, dst, sem)
    copy.start()
    return copy


def right_kernel(dims, x_hbm, w_hbm, out_hbm, x_ref, w_ref, out_ref, w_sem, in_sem, out_sem):
    w_copy = fetch(w_hbm, w_ref, w_sem)
    wide = PAIR * BIN
    x_copies = []
    for p in range(OWNED // PAIR):
        cols = pl.ds(p * wide, wide)
        x_copies.append(fetch(x_hbm.at[:, cols], x_ref.at[:, cols], in_sem.at[p]))
    w_copy.wait()
    out_copies = []
    for p in range(OWNED // PAIR):
        x_copies[p].wait()
        for k in range(p * PAIR, (p + 1) * PAIR):
            value = dot(w_ref[k], x_ref[:, k * BIN : (k + 1) * BIN], dims).astype(BF16)
            scatter_rows(out_ref, k, value)
        rows = pl.ds(p * PAIR * PIECE, PAIR * PIECE)
        out_copies.append(fetch(out_ref.at[:, rows, :], out_hbm.at[:, rows, :], out_sem.at[p]))
    for copy in out_copies:
        copy.wait()


def up_kernel(place_ref, msg_ref, left_ref, down_ref, out_ref, saved_ref, slope_ref, held_ref, shard_ref):
    j = pl.program_id(0)

    @pl.when(j == 0)
    def _():
        gather_rows(msg_ref, held_ref)
        shard_ref[...] = shard_matrix(place_ref[0])

    v = held_ref[j]
    saved_ref[0] = dot(shard_ref[...], v, NN).astype(BF16)
    s = dot(left_ref[0], v, TN)
    c = math.sqrt(2.0 / math.pi)
    square = s * s
    th = jnp.tanh(s * (c + (c * 0.044715) * square))
    half = 0.5 + 0.5 * th
    hidden = (s * half).astype(BF16)
    slope = half + (0.5 * s) * ((1.0 - th * th) * (c + (3.0 * c * 0.044715) * square))
    slope_ref[0] = slope.astype(BF16)
    z = dot(down_ref[0], hidden, TN).astype(BF16)
    scatter_rows(out_ref, 0, z)


def back_kernel(msg_ref, saved_ref, slope_ref, left_ref, down_ref, out_ref, send_ref, keep_ref, held_ref):
    j = pl.program_id(0)

    @pl.when(j == 0)
    def _():
        gather_rows(msg_ref, held_ref)

    grad_hidden = dot(down_ref[0], held_ref[j], NN)
    grad_pre = (grad_hidden * slope_ref[0].astype(F32)).astype(BF16)
    grad_v = dot(left_ref[0], grad_pre, NN).astype(BF16)
    scatter_rows(out_ref, 0, grad_v)
    part = dot(saved_ref[0], grad_pre, NT)
    send_ref[...] = part[: BIN // 2].astype(BF16)
    keep_ref[...] = part[BIN // 2 :]


def out_kernel(
    place_ref, msg_ref, left_hbm, cot_hbm, out_hbm, send_ref, keep_ref,
    held_ref, left_ref, cot_ref, out_ref, left_sem, in_sem, out_sem,
):
    wide = PAIR * BIN
    cot_copy = fetch(cot_hbm, cot_ref, in_sem)
    left_copy = fetch(left_hbm, left_ref, left_sem)
    shard = shard_matrix(place_ref[0])
    gather_rows(msg_ref, held_ref)
    left_copy.wait()
    cot_copy.wait()
    out_copies = []
    for p in range(OWNED // PAIR):
        for k in range(p * PAIR, (p + 1) * PAIR):
            cols = slice(k * BIN, (k + 1) * BIN)
            w = held_ref[k]
            out_ref[:, cols] = dot(w, left_ref[k], TN).astype(BF16)
            part = dot(dot(shard, w, NN).astype(BF16), cot_ref[:, cols], NN)
            send_ref[:, cols] = part[: BIN // 2].astype(BF16)
            keep_ref[:, cols] = part[BIN // 2 :]
        cols = pl.ds(p * wide, wide)
        out_copies.append(fetch(out_ref.at[:, cols], out_hbm.at[:, cols], out_sem.at[p]))
    for copy in out_copies:
        copy.wait()


def in_kernel(msg_ref, right_hbm, out_hbm, held_ref, right_ref, out_ref, right_sem, out_sem):
    wide = PAIR * BIN
    right_copy = fetch(right_hbm, right_ref, right_sem)
    gather_rows(msg_ref, held_ref)
    right_copy.wait()
    out_copies = []
    for p in range(OWNED // PAIR):
        for k in range(p * PAIR, (p + 1) * PAIR):
            out_ref[:, k * BIN : (k + 1) * BIN] = dot(held_ref[k], right_ref[k], TT).astype(BF16)
        cols = pl.ds(p * wide, wide)
        out_copies.append(fetch(out_ref.at[:, cols], out_hbm.at[:, cols], out_sem.at[p]))
    for copy in out_copies:
        copy.wait()


VMEM = pl.BlockSpec(memory_space=pltpu.VMEM)
SMEM = pl.BlockSpec(memory_space=pltpu.SMEM)
MSG = (GROUPS, BIN, ROWS)


def params(mib):
    return pltpu.CompilerParams(vmem_limit_bytes=mib * MIB)


def cost(mflop, mib, trans=0):
    return pl.CostEstimate(flops=mflop * 1000000, bytes_accessed=mib * MIB, transcendentals=trans)


def shape(dims, dtype):
    return jax.ShapeDtypeStruct(dims, dtype)


def far(dims, dtype):
    return pltpu.HBM(dims, dtype)


def stay(x):
    return pltpu.with_memory_space_constraint(x, pltpu.HBM)


def each(dims, count=1):
    return pl.BlockSpec((count,) + dims, lambda j: (j, 0, 0))


def pieces(count):
    return pl.BlockSpec((GROUPS, count * PIECE, ROWS), lambda j: (0, j, 0))


def columns(rows, width):
    return pl.BlockSpec((rows, width), lambda j: (0, j))


HELD = pltpu.VMEM((OWNED, BIN, ROWS), BF16)
SHARD = pltpu.VMEM((BIN, BIN), BF16)


ANY = pl.BlockSpec(memory_space=pl.ANY)
SQUARES = pltpu.VMEM((OWNED, BIN, BIN), BF16)
FLAT = pltpu.VMEM((ROWS, OWNED * BIN), BF16)
ONE = pltpu.SemaphoreType.DMA
SEMS = pltpu.SemaphoreType.DMA((OWNED // PAIR,))


def right(x, w, dims):
    return pl.pallas_call(
        functools.partial(right_kernel, dims),
        out_shape=far(MSG, BF16),
        in_specs=[ANY, ANY],
        out_specs=ANY,
        scratch_shapes=[FLAT, SQUARES, pltpu.VMEM(MSG, BF16), ONE, SEMS, SEMS],
        compiler_params=params(16),
        cost_estimate=cost(134, 3),
    )(stay(x), stay(w))


def up(place, msg, left, down):
    return pl.pallas_call(
        up_kernel,
        grid=(OWNED,),
        out_shape=[far(MSG, BF16), far((OWNED, BIN, ROWS), BF16), far((OWNED, BHID, ROWS), BF16)],
        in_specs=[SMEM, VMEM, each((BIN, BHID)), each((BHID, BIN))],
        out_specs=[pieces(1), each((BIN, ROWS)), each((BHID, ROWS))],
        scratch_shapes=[HELD, SHARD],
        compiler_params=params(24),
        cost_estimate=cost(1300, 9, OWNED * BHID * ROWS),
    )(place, msg, stay(left), stay(down))


def back(msg, saved, slope, left, down):
    half = (BIN // 2, OWNED * BHID)
    return pl.pallas_call(
        back_kernel,
        grid=(OWNED,),
        out_shape=[far(MSG, BF16), far(half, BF16), far(half, F32)],
        in_specs=[VMEM, each((BIN, ROWS)), each((BHID, ROWS)), each((BIN, BHID)), each((BHID, BIN))],
        out_specs=[pieces(1), columns(BIN // 2, BHID), columns(BIN // 2, BHID)],
        scratch_shapes=[HELD],
        compiler_params=params(24),
        cost_estimate=cost(1800, 11),
    )(msg, stay(saved), stay(slope), stay(left), stay(down))


def out(place, msg, left, cot):
    half = (BIN // 2, OWNED * BIN)
    return pl.pallas_call(
        out_kernel,
        out_shape=[far((ROWS, OWNED * BIN), BF16), far(half, BF16), far(half, F32)],
        in_specs=[SMEM, VMEM, ANY, ANY],
        out_specs=[ANY, VMEM, VMEM],
        scratch_shapes=[HELD, SQUARES, FLAT, FLAT, ONE, ONE, SEMS],
        compiler_params=params(20),
        cost_estimate=cost(3000, 16),
    )(place, msg, stay(left), stay(cot))


def into(msg, rightw):
    return pl.pallas_call(
        in_kernel,
        out_shape=far((ROWS, OWNED * BIN), BF16),
        in_specs=[VMEM, ANY],
        out_specs=ANY,
        scratch_shapes=[HELD, SQUARES, FLAT, ONE, SEMS],
        compiler_params=params(20),
        cost_estimate=cost(300, 3),
    )(msg, stay(rightw))


def exchange(msg):
    return lax.all_to_all(msg, "blk", split_axis=0, concat_axis=0, tiled=True)


def join_kernel(up_keep_ref, up_far_ref, down_keep_ref, down_far_ref, out_ref):
    at = 0
    for kept, far_ref in ((up_keep_ref, up_far_ref), (down_keep_ref, down_far_ref)):
        cols = slice(at, at + kept.shape[1])
        at += kept.shape[1]
        total = (kept[...] + far_ref[...].astype(F32)).astype(BF16)
        for n in range(out_ref.shape[0]):
            out_ref[n, :, cols] = total[2 * n : 2 * n + 2]


def join(up_keep, up_far, down_keep, down_far):
    dims = (up_keep.shape[0] // 2, 2, up_keep.shape[1] + down_keep.shape[1])
    return pl.pallas_call(
        join_kernel,
        out_shape=shape(dims, BF16),
        in_specs=[VMEM] * 4,
        out_specs=VMEM,
        compiler_params=params(8),
        cost_estimate=cost(1, 1),
    )(up_keep, up_far, down_keep, down_far)


def axis_of(bit):
    return DP[len(DP) - 1 - bit]


def swap_halves(send, step):
    return lax.ppermute(send, axis_of(STEPS[step]), [(0, 1), (1, 0)])


def halve(send, keep, step):
    total = keep + swap_halves(send, step).astype(F32)
    rows = total.shape[0] // 2
    return total[:rows].astype(BF16), total[rows:]


def finish_kernel(factor, in_ref, up_ref, down_ref):
    total = in_ref[0].astype(F32)
    for n in range(1, in_ref.shape[0]):
        total = total + in_ref[n].astype(F32)
    total = total * factor
    at = 0
    for ref in (up_ref, down_ref):
        for k in range(OWNED):
            ref[k] = total[:, at : at + ref.shape[2]]
            at += ref.shape[2]


def finish(pieces_in, factor):
    rows = pieces_in.shape[1]
    return pl.pallas_call(
        functools.partial(finish_kernel, factor),
        out_shape=[shape((OWNED, rows, BHID), F32), shape((OWNED, rows, BIN), F32)],
        in_specs=[VMEM],
        out_specs=[VMEM] * 2,
        compiler_params=params(8),
        cost_estimate=cost(1, 1),
    )(pieces_in)


def sum_over_dp(up_half, down_half, grad_u, factor):
    for step in range(len(STEPS) - 1):
        up_half = halve(*up_half, step)
        down_half = halve(*down_half, step)
    last = len(STEPS) - 1
    total = join(up_half[1], swap_halves(up_half[0], last), down_half[1], swap_halves(down_half[0], last))
    total, grad_u = lax.optimization_barrier((total, grad_u))
    total = lax.all_to_all(total, tuple(axis_of(bit) for bit in SHARED), 0, 0, tiled=True)
    return (*finish(total, factor), grad_u)


def on_device(tokens, up_right, up_left, down_right, down_left, cotangent):
    place = lax.axis_index(DP).reshape(1).astype(jnp.int32)
    factor = 1.0 / math.sqrt(tokens.shape[0] * lax.axis_size(DP))
    v = exchange(right(tokens, up_right, TT))
    grad_z = exchange(right(cotangent, down_left, NT))
    z, saved, slope = up(place, v, up_left, down_right)
    w = exchange(z)
    grad_v, up_send, up_keep = back(grad_z, saved, slope, up_left, down_right)
    grad_u = exchange(grad_v)
    layer_out, down_send, down_keep = out(place, w, down_left, cotangent)
    up_grad, down_grad, grad_u = sum_over_dp((up_send, up_keep), (down_send, down_keep), grad_u, factor)
    input_grad = into(grad_u, up_right)
    return (layer_out, input_grad, up_grad, down_grad)


def solution(mesh):
    fine = jax.sharding.Mesh(mesh.devices.reshape((2,) * len(DP) + (GROUPS,)), DP + ("blk",))
    placed = (
        P(DP, "blk"),
        P("blk", None, None),
        P("blk", None, None),
        P("blk", None, None),
        P("blk", None, None),
        P(DP, "blk"),
    )
    return jax.shard_map(
        on_device,
        mesh=fine,
        in_specs=placed,
        out_specs=(P(DP, "blk"), P(DP, "blk"), P("blk", DP, None), P("blk", DP, None)),
        check_vma=False,
    )
```

```python
import functools
import math

import jax
import jax.numpy as jnp
from jax import lax
from jax.experimental import pallas as pl
from jax.experimental.pallas import tpu as pltpu
from jax.sharding import PartitionSpec as P

GROUPS = 8
OWNED = 8
BIN = 128
BHID = 512
ROWS = 512
PIECE = 16
PAIR = 2
UP_STEPS = (2, 0, 3)
DOWN_STEPS = (0, 2, 3)
SHARED = (5, 4, 1)
DP = ("z8", "z4", "z2", "z1", "far", "core")
MIB = 1 << 20
BF16 = jnp.bfloat16
F32 = jnp.float32

NN = (((1,), (0,)), ((), ()))
NT = (((1,), (1,)), ((), ()))
TN = (((0,), (0,)), ((), ()))
TT = (((0,), (1,)), ((), ()))


def dot(a, b, dims):
    return lax.dot_general(a, b, dims, preferred_element_type=F32)


def swap_matrix():
    to = lax.broadcasted_iota(jnp.int32, (BIN, BIN), 0)
    come = lax.broadcasted_iota(jnp.int32, (BIN, BIN), 1)
    wanted = ((to & 14) << 3) | ((to >> 4) << 1) | (to & 1)
    return jnp.where(come == wanted, 1.0, 0.0).astype(BF16)


def shard_matrix(steps, place):
    to = lax.broadcasted_iota(jnp.int32, (BIN, BIN), 0)
    come = lax.broadcasted_iota(jnp.int32, (BIN, BIN), 1)
    owner = jnp.zeros_like(to)
    for at, bit in enumerate(steps + SHARED):
        here = (to >> (len(steps + SHARED) - at)) & 1
        if bit in steps:
            here = (1 - here) ^ ((place >> bit) & 1)
        owner = owner | (here << bit)
    return jnp.where(come == ((owner << 1) | (to & 1)), 1.0, 0.0).astype(BF16)


def scatter_rows(out_ref, slot, value):
    for n in range(GROUPS):
        out_ref[n, slot * PIECE : (slot + 1) * PIECE, :] = value[n * PIECE : (n + 1) * PIECE, :]


def gather_rows(msg_ref, held_ref):
    swap = swap_matrix()
    for src in range(GROUPS):
        swapped = dot(swap, msg_ref[src], NN).astype(BF16)
        for b in range(OWNED):
            held_ref[b, src * PIECE : (src + 1) * PIECE, :] = swapped[b * PIECE : (b + 1) * PIECE, :]


def fetch(src, dst, sem):
    copy = pltpu.make_async_copy(src, dst, sem)
    copy.start()
    return copy


def right_kernel(dims, x_hbm, w_hbm, out_hbm, x_ref, w_ref, out_ref, w_sem, in_sem, out_sem):
    w_copy = fetch(w_hbm, w_ref, w_sem)
    wide = PAIR * BIN
    x_copies = []
    for p in range(OWNED // PAIR):
        cols = pl.ds(p * wide, wide)
        x_copies.append(fetch(x_hbm.at[:, cols], x_ref.at[:, cols], in_sem.at[p]))
    w_copy.wait()
    out_copies = []
    for p in range(OWNED // PAIR):
        x_copies[p].wait()
        for k in range(p * PAIR, (p + 1) * PAIR):
            value = dot(w_ref[k], x_ref[:, k * BIN : (k + 1) * BIN], dims).astype(BF16)
            scatter_rows(out_ref, k, value)
        rows = pl.ds(p * PAIR * PIECE, PAIR * PIECE)
        out_copies.append(fetch(out_ref.at[:, rows, :], out_hbm.at[:, rows, :], out_sem.at[p]))
    for copy in out_copies:
        copy.wait()


def up_kernel(place_ref, msg_ref, left_ref, down_ref, out_ref, saved_ref, slope_ref, held_ref, shard_ref):
    j = pl.program_id(0)

    @pl.when(j == 0)
    def _():
        gather_rows(msg_ref, held_ref)
        shard_ref[...] = shard_matrix(UP_STEPS, place_ref[0])

    v = held_ref[j]
    saved_ref[0] = dot(shard_ref[...], v, NN).astype(BF16)
    s = dot(left_ref[0], v, TN)
    c = math.sqrt(2.0 / math.pi)
    square = s * s
    th = jnp.tanh(s * (c + (c * 0.044715) * square))
    half = 0.5 + 0.5 * th
    hidden = (s * half).astype(BF16)
    slope = half + (0.5 * s) * ((1.0 - th * th) * (c + (3.0 * c * 0.044715) * square))
    slope_ref[0] = slope.astype(BF16)
    z = dot(down_ref[0], hidden, TN).astype(BF16)
    scatter_rows(out_ref, 0, z)


def back_kernel(msg_ref, saved_ref, slope_ref, left_ref, down_ref, out_ref, send_ref, keep_ref, held_ref):
    j = pl.program_id(0)

    @pl.when(j == 0)
    def _():
        gather_rows(msg_ref, held_ref)

    grad_hidden = dot(down_ref[0], held_ref[j], NN)
    grad_pre = (grad_hidden * slope_ref[0].astype(F32)).astype(BF16)
    grad_v = dot(left_ref[0], grad_pre, NN).astype(BF16)
    scatter_rows(out_ref, 0, grad_v)
    part = dot(saved_ref[0], grad_pre, NT)
    send_ref[...] = part[: BIN // 2].astype(BF16)
    keep_ref[...] = part[BIN // 2 :]


def out_kernel(
    place_ref, msg_ref, left_hbm, cot_hbm, out_hbm, send_ref, keep_ref,
    held_ref, left_ref, cot_ref, out_ref, left_sem, in_sem, out_sem,
):
    wide = PAIR * BIN
    cot_copy = fetch(cot_hbm, cot_ref, in_sem)
    left_copy = fetch(left_hbm, left_ref, left_sem)
    shard = shard_matrix(DOWN_STEPS, place_ref[0])
    gather_rows(msg_ref, held_ref)
    left_copy.wait()
    cot_copy.wait()
    out_copies = []
    for p in range(OWNED // PAIR):
        for k in range(p * PAIR, (p + 1) * PAIR):
            cols = slice(k * BIN, (k + 1) * BIN)
            w = held_ref[k]
            out_ref[:, cols] = dot(w, left_ref[k], TN).astype(BF16)
            part = dot(dot(shard, w, NN).astype(BF16), cot_ref[:, cols], NN)
            send_ref[:, cols] = part[: BIN // 2].astype(BF16)
            keep_ref[:, cols] = part[BIN // 2 :]
        cols = pl.ds(p * wide, wide)
        out_copies.append(fetch(out_ref.at[:, cols], out_hbm.at[:, cols], out_sem.at[p]))
    for copy in out_copies:
        copy.wait()


def in_kernel(msg_ref, right_hbm, out_hbm, held_ref, right_ref, out_ref, right_sem, out_sem):
    wide = PAIR * BIN
    right_copy = fetch(right_hbm, right_ref, right_sem)
    gather_rows(msg_ref, held_ref)
    right_copy.wait()
    out_copies = []
    for p in range(OWNED // PAIR):
        for k in range(p * PAIR, (p + 1) * PAIR):
            out_ref[:, k * BIN : (k + 1) * BIN] = dot(held_ref[k], right_ref[k], TT).astype(BF16)
        cols = pl.ds(p * wide, wide)
        out_copies.append(fetch(out_ref.at[:, cols], out_hbm.at[:, cols], out_sem.at[p]))
    for copy in out_copies:
        copy.wait()


VMEM = pl.BlockSpec(memory_space=pltpu.VMEM)
SMEM = pl.BlockSpec(memory_space=pltpu.SMEM)
MSG = (GROUPS, BIN, ROWS)


def params(mib):
    return pltpu.CompilerParams(vmem_limit_bytes=mib * MIB)


def cost(mflop, mib, trans=0):
    return pl.CostEstimate(flops=mflop * 1000000, bytes_accessed=mib * MIB, transcendentals=trans)


def shape(dims, dtype):
    return jax.ShapeDtypeStruct(dims, dtype)


def far(dims, dtype):
    return pltpu.HBM(dims, dtype)


def stay(x):
    return pltpu.with_memory_space_constraint(x, pltpu.HBM)


def each(dims, count=1):
    return pl.BlockSpec((count,) + dims, lambda j: (j, 0, 0))


def pieces(count):
    return pl.BlockSpec((GROUPS, count * PIECE, ROWS), lambda j: (0, j, 0))


def columns(rows, width):
    return pl.BlockSpec((rows, width), lambda j: (0, j))


HELD = pltpu.VMEM((OWNED, BIN, ROWS), BF16)
SHARD = pltpu.VMEM((BIN, BIN), BF16)


ANY = pl.BlockSpec(memory_space=pl.ANY)
SQUARES = pltpu.VMEM((OWNED, BIN, BIN), BF16)
FLAT = pltpu.VMEM((ROWS, OWNED * BIN), BF16)
ONE = pltpu.SemaphoreType.DMA
SEMS = pltpu.SemaphoreType.DMA((OWNED // PAIR,))


def right(x, w, dims):
    return pl.pallas_call(
        functools.partial(right_kernel, dims),
        out_shape=far(MSG, BF16),
        in_specs=[ANY, ANY],
        out_specs=ANY,
        scratch_shapes=[FLAT, SQUARES, pltpu.VMEM(MSG, BF16), ONE, SEMS, SEMS],
        compiler_params=params(16),
        cost_estimate=cost(134, 3),
    )(stay(x), stay(w))


def up(place, msg, left, down):
    return pl.pallas_call(
        up_kernel,
        grid=(OWNED,),
        out_shape=[far(MSG, BF16), far((OWNED, BIN, ROWS), BF16), far((OWNED, BHID, ROWS), BF16)],
        in_specs=[SMEM, VMEM, each((BIN, BHID)), each((BHID, BIN))],
        out_specs=[pieces(1), each((BIN, ROWS)), each((BHID, ROWS))],
        scratch_shapes=[HELD, SHARD],
        compiler_params=params(24),
        cost_estimate=cost(1300, 9, OWNED * BHID * ROWS),
    )(place, msg, stay(left), stay(down))


def back(msg, saved, slope, left, down):
    half = (BIN // 2, OWNED * BHID)
    return pl.pallas_call(
        back_kernel,
        grid=(OWNED,),
        out_shape=[far(MSG, BF16), far(half, BF16), far(half, F32)],
        in_specs=[VMEM, each((BIN, ROWS)), each((BHID, ROWS)), each((BIN, BHID)), each((BHID, BIN))],
        out_specs=[pieces(1), columns(BIN // 2, BHID), columns(BIN // 2, BHID)],
        scratch_shapes=[HELD],
        compiler_params=params(24),
        cost_estimate=cost(1800, 11),
    )(msg, stay(saved), stay(slope), stay(left), stay(down))


def out(place, msg, left, cot):
    half = (BIN // 2, OWNED * BIN)
    return pl.pallas_call(
        out_kernel,
        out_shape=[far((ROWS, OWNED * BIN), BF16), shape(half, BF16), shape(half, F32)],
        in_specs=[SMEM, VMEM, ANY, ANY],
        out_specs=[ANY, VMEM, VMEM],
        scratch_shapes=[HELD, SQUARES, FLAT, FLAT, ONE, ONE, SEMS],
        compiler_params=params(20),
        cost_estimate=cost(3000, 16),
    )(place, msg, stay(left), stay(cot))


def into(msg, rightw):
    return pl.pallas_call(
        in_kernel,
        out_shape=far((ROWS, OWNED * BIN), BF16),
        in_specs=[VMEM, ANY],
        out_specs=ANY,
        scratch_shapes=[HELD, SQUARES, FLAT, ONE, SEMS],
        compiler_params=params(20),
        cost_estimate=cost(300, 3),
    )(msg, stay(rightw))


def exchange(msg):
    return lax.all_to_all(msg, "blk", split_axis=0, concat_axis=0, tiled=True)


def join_kernel(up_keep_ref, up_far_ref, down_keep_ref, down_far_ref, out_ref):
    at = 0
    for kept, far_ref in ((up_keep_ref, up_far_ref), (down_keep_ref, down_far_ref)):
        cols = slice(at, at + kept.shape[1])
        at += kept.shape[1]
        total = (kept[...] + far_ref[...].astype(F32)).astype(BF16)
        for n in range(out_ref.shape[0]):
            out_ref[n, :, cols] = total[2 * n : 2 * n + 2]


def join(up_keep, up_far, down_keep, down_far):
    dims = (up_keep.shape[0] // 2, 2, up_keep.shape[1] + down_keep.shape[1])
    return pl.pallas_call(
        join_kernel,
        out_shape=shape(dims, BF16),
        in_specs=[VMEM] * 4,
        out_specs=VMEM,
        compiler_params=params(8),
        cost_estimate=cost(1, 1),
    )(up_keep, up_far, down_keep, down_far)


def axis_of(bit):
    return DP[len(DP) - 1 - bit]


def swap_halves(send, bit):
    return lax.ppermute(send, axis_of(bit), [(0, 1), (1, 0)])


def halve(send, keep, bit):
    total = keep + swap_halves(send, bit).astype(F32)
    rows = total.shape[0] // 2
    return total[:rows].astype(BF16), total[rows:]


def finish_kernel(factor, in_ref, up_ref, down_ref):
    total = in_ref[0].astype(F32)
    for n in range(1, in_ref.shape[0]):
        total = total + in_ref[n].astype(F32)
    total = total * factor
    at = 0
    for ref in (up_ref, down_ref):
        for k in range(OWNED):
            ref[k] = total[:, at : at + ref.shape[2]]
            at += ref.shape[2]


def finish(pieces_in, factor):
    rows = pieces_in.shape[1]
    return pl.pallas_call(
        functools.partial(finish_kernel, factor),
        out_shape=[shape((OWNED, rows, BHID), F32), shape((OWNED, rows, BIN), F32)],
        in_specs=[VMEM],
        out_specs=[VMEM] * 2,
        compiler_params=params(8),
        cost_estimate=cost(1, 1),
    )(pieces_in)


def sum_over_dp(up_half, down_half, grad_u, factor):
    for bit in UP_STEPS[:-1]:
        up_half = halve(*up_half, bit)
    for bit in DOWN_STEPS[:-1]:
        down_half = halve(*down_half, bit)
    up_send, up_keep = up_half
    down_send, down_keep = down_half
    down_send, grad_u = lax.optimization_barrier((down_send, grad_u))
    up_far, down_far = swap_halves(up_send, UP_STEPS[-1]), swap_halves(down_send, DOWN_STEPS[-1])
    total = join(up_keep, up_far, down_keep, down_far)
    total = lax.all_to_all(total, tuple(axis_of(bit) for bit in SHARED), 0, 0, tiled=True)
    return (*finish(total, factor), grad_u)


def on_device(tokens, up_right, up_left, down_right, down_left, cotangent):
    place = lax.axis_index(DP).reshape(1).astype(jnp.int32)
    factor = 1.0 / math.sqrt(tokens.shape[0] * lax.axis_size(DP))
    v = exchange(right(tokens, up_right, TT))
    grad_z = exchange(right(cotangent, down_left, NT))
    z, saved, slope = up(place, v, up_left, down_right)
    w = exchange(z)
    grad_v, up_send, up_keep = back(grad_z, saved, slope, up_left, down_right)
    grad_u = exchange(grad_v)
    layer_out, down_send, down_keep = out(place, w, down_left, cotangent)
    up_grad, down_grad, grad_u = sum_over_dp((up_send, up_keep), (down_send, down_keep), grad_u, factor)
    input_grad = into(grad_u, up_right)
    return (layer_out, input_grad, up_grad, down_grad)


def solution(mesh):
    fine = jax.sharding.Mesh(mesh.devices.reshape((2,) * len(DP) + (GROUPS,)), DP + ("blk",))
    placed = (
        P(DP, "blk"),
        P("blk", None, None),
        P("blk", None, None),
        P("blk", None, None),
        P("blk", None, None),
        P(DP, "blk"),
    )
    return jax.shard_map(
        on_device,
        mesh=fine,
        in_specs=placed,
        out_specs=(P(DP, "blk"), P(DP, "blk"), P("blk", DP, None), P("blk", DP, None)),
        check_vma=False,
    )
```

```python
import functools
import math

import jax
import jax.numpy as jnp
from jax import lax
from jax.experimental import pallas as pl
from jax.experimental.pallas import tpu as pltpu
from jax.sharding import PartitionSpec as P

GROUPS = 8
OWNED = 8
BIN = 128
BHID = 512
ROWS = 512
PIECE = 16
PAIR = 2
UP_STEPS = (2, 0)
DOWN_STEPS = (0, 2)
SHARED = (5, 4, 3, 1)
DP = ("z8", "z4", "z2", "z1", "far", "core")
MIB = 1 << 20
BF16 = jnp.bfloat16
F32 = jnp.float32

NN = (((1,), (0,)), ((), ()))
NT = (((1,), (1,)), ((), ()))
TN = (((0,), (0,)), ((), ()))
TT = (((0,), (1,)), ((), ()))


def dot(a, b, dims):
    return lax.dot_general(a, b, dims, preferred_element_type=F32)


def swap_matrix():
    to = lax.broadcasted_iota(jnp.int32, (BIN, BIN), 0)
    come = lax.broadcasted_iota(jnp.int32, (BIN, BIN), 1)
    wanted = ((to & 14) << 3) | ((to >> 4) << 1) | (to & 1)
    return jnp.where(come == wanted, 1.0, 0.0).astype(BF16)


def shard_matrix(steps, place):
    to = lax.broadcasted_iota(jnp.int32, (BIN, BIN), 0)
    come = lax.broadcasted_iota(jnp.int32, (BIN, BIN), 1)
    owner = jnp.zeros_like(to)
    for at, bit in enumerate(steps + SHARED):
        here = (to >> (len(steps + SHARED) - at)) & 1
        if bit in steps:
            here = (1 - here) ^ ((place >> bit) & 1)
        owner = owner | (here << bit)
    return jnp.where(come == ((owner << 1) | (to & 1)), 1.0, 0.0).astype(BF16)


def scatter_rows(out_ref, slot, value):
    for n in range(GROUPS):
        out_ref[n, slot * PIECE : (slot + 1) * PIECE, :] = value[n * PIECE : (n + 1) * PIECE, :]


def gather_rows(msg_ref, held_ref):
    swap = swap_matrix()
    for src in range(GROUPS):
        swapped = dot(swap, msg_ref[src], NN).astype(BF16)
        for b in range(OWNED):
            held_ref[b, src * PIECE : (src + 1) * PIECE, :] = swapped[b * PIECE : (b + 1) * PIECE, :]


def fetch(src, dst, sem):
    copy = pltpu.make_async_copy(src, dst, sem)
    copy.start()
    return copy


def right_kernel(dims, x_hbm, w_hbm, out_hbm, x_ref, w_ref, out_ref, w_sem, in_sem, out_sem):
    w_copy = fetch(w_hbm, w_ref, w_sem)
    wide = PAIR * BIN
    x_copies = []
    for p in range(OWNED // PAIR):
        cols = pl.ds(p * wide, wide)
        x_copies.append(fetch(x_hbm.at[:, cols], x_ref.at[:, cols], in_sem.at[p]))
    w_copy.wait()
    out_copies = []
    for p in range(OWNED // PAIR):
        x_copies[p].wait()
        for k in range(p * PAIR, (p + 1) * PAIR):
            value = dot(w_ref[k], x_ref[:, k * BIN : (k + 1) * BIN], dims).astype(BF16)
            scatter_rows(out_ref, k, value)
        rows = pl.ds(p * PAIR * PIECE, PAIR * PIECE)
        out_copies.append(fetch(out_ref.at[:, rows, :], out_hbm.at[:, rows, :], out_sem.at[p]))
    for copy in out_copies:
        copy.wait()


def up_kernel(place_ref, msg_ref, left_ref, down_ref, out_ref, saved_ref, slope_ref, held_ref, shard_ref):
    j = pl.program_id(0)

    @pl.when(j == 0)
    def _():
        gather_rows(msg_ref, held_ref)
        shard_ref[...] = shard_matrix(UP_STEPS, place_ref[0])

    v = held_ref[j]
    saved_ref[0] = dot(shard_ref[...], v, NN).astype(BF16)
    s = dot(left_ref[0], v, TN)
    c = math.sqrt(2.0 / math.pi)
    square = s * s
    th = jnp.tanh(s * (c + (c * 0.044715) * square))
    half = 0.5 + 0.5 * th
    hidden = (s * half).astype(BF16)
    slope = half + (0.5 * s) * ((1.0 - th * th) * (c + (3.0 * c * 0.044715) * square))
    slope_ref[0] = slope.astype(BF16)
    z = dot(down_ref[0], hidden, TN).astype(BF16)
    scatter_rows(out_ref, 0, z)


def back_kernel(msg_ref, saved_ref, slope_ref, left_ref, down_ref, out_ref, send_ref, keep_ref, held_ref):
    j = pl.program_id(0)

    @pl.when(j == 0)
    def _():
        gather_rows(msg_ref, held_ref)

    grad_hidden = dot(down_ref[0], held_ref[j], NN)
    grad_pre = (grad_hidden * slope_ref[0].astype(F32)).astype(BF16)
    grad_v = dot(left_ref[0], grad_pre, NN).astype(BF16)
    scatter_rows(out_ref, 0, grad_v)
    part = dot(saved_ref[0], grad_pre, NT)
    send_ref[...] = part[: BIN // 2].astype(BF16)
    keep_ref[...] = part[BIN // 2 :]


def out_kernel(
    place_ref, msg_ref, left_hbm, cot_hbm, out_hbm, send_ref, keep_ref,
    held_ref, left_ref, cot_ref, out_ref, left_sem, in_sem, out_sem,
):
    wide = PAIR * BIN
    cot_copy = fetch(cot_hbm, cot_ref, in_sem)
    left_copy = fetch(left_hbm, left_ref, left_sem)
    shard = shard_matrix(DOWN_STEPS, place_ref[0])
    gather_rows(msg_ref, held_ref)
    left_copy.wait()
    cot_copy.wait()
    out_copies = []
    for p in range(OWNED // PAIR):
        for k in range(p * PAIR, (p + 1) * PAIR):
            cols = slice(k * BIN, (k + 1) * BIN)
            w = held_ref[k]
            out_ref[:, cols] = dot(w, left_ref[k], TN).astype(BF16)
            part = dot(dot(shard, w, NN).astype(BF16), cot_ref[:, cols], NN)
            send_ref[:, cols] = part[: BIN // 2].astype(BF16)
            keep_ref[:, cols] = part[BIN // 2 :]
        cols = pl.ds(p * wide, wide)
        out_copies.append(fetch(out_ref.at[:, cols], out_hbm.at[:, cols], out_sem.at[p]))
    for copy in out_copies:
        copy.wait()


def in_kernel(msg_ref, right_hbm, out_hbm, held_ref, right_ref, out_ref, right_sem, out_sem):
    wide = PAIR * BIN
    right_copy = fetch(right_hbm, right_ref, right_sem)
    gather_rows(msg_ref, held_ref)
    right_copy.wait()
    out_copies = []
    for p in range(OWNED // PAIR):
        for k in range(p * PAIR, (p + 1) * PAIR):
            out_ref[:, k * BIN : (k + 1) * BIN] = dot(held_ref[k], right_ref[k], TT).astype(BF16)
        cols = pl.ds(p * wide, wide)
        out_copies.append(fetch(out_ref.at[:, cols], out_hbm.at[:, cols], out_sem.at[p]))
    for copy in out_copies:
        copy.wait()


VMEM = pl.BlockSpec(memory_space=pltpu.VMEM)
SMEM = pl.BlockSpec(memory_space=pltpu.SMEM)
MSG = (GROUPS, BIN, ROWS)


def params(mib):
    return pltpu.CompilerParams(vmem_limit_bytes=mib * MIB)


def cost(mflop, mib, trans=0):
    return pl.CostEstimate(flops=mflop * 1000000, bytes_accessed=mib * MIB, transcendentals=trans)


def shape(dims, dtype):
    return jax.ShapeDtypeStruct(dims, dtype)


def far(dims, dtype):
    return pltpu.HBM(dims, dtype)


def stay(x):
    return pltpu.with_memory_space_constraint(x, pltpu.HBM)


def each(dims, count=1):
    return pl.BlockSpec((count,) + dims, lambda j: (j, 0, 0))


def pieces(count):
    return pl.BlockSpec((GROUPS, count * PIECE, ROWS), lambda j: (0, j, 0))


def columns(rows, width):
    return pl.BlockSpec((rows, width), lambda j: (0, j))


HELD = pltpu.VMEM((OWNED, BIN, ROWS), BF16)
SHARD = pltpu.VMEM((BIN, BIN), BF16)


ANY = pl.BlockSpec(memory_space=pl.ANY)
SQUARES = pltpu.VMEM((OWNED, BIN, BIN), BF16)
FLAT = pltpu.VMEM((ROWS, OWNED * BIN), BF16)
ONE = pltpu.SemaphoreType.DMA
SEMS = pltpu.SemaphoreType.DMA((OWNED // PAIR,))


def right(x, w, dims):
    return pl.pallas_call(
        functools.partial(right_kernel, dims),
        out_shape=far(MSG, BF16),
        in_specs=[ANY, ANY],
        out_specs=ANY,
        scratch_shapes=[FLAT, SQUARES, pltpu.VMEM(MSG, BF16), ONE, SEMS, SEMS],
        compiler_params=params(16),
        cost_estimate=cost(134, 3),
    )(stay(x), stay(w))


def up(place, msg, left, down):
    return pl.pallas_call(
        up_kernel,
        grid=(OWNED,),
        out_shape=[far(MSG, BF16), far((OWNED, BIN, ROWS), BF16), far((OWNED, BHID, ROWS), BF16)],
        in_specs=[SMEM, VMEM, each((BIN, BHID)), each((BHID, BIN))],
        out_specs=[pieces(1), each((BIN, ROWS)), each((BHID, ROWS))],
        scratch_shapes=[HELD, SHARD],
        compiler_params=params(24),
        cost_estimate=cost(1300, 9, OWNED * BHID * ROWS),
    )(place, msg, stay(left), stay(down))


def back(msg, saved, slope, left, down):
    half = (BIN // 2, OWNED * BHID)
    return pl.pallas_call(
        back_kernel,
        grid=(OWNED,),
        out_shape=[far(MSG, BF16), far(half, BF16), far(half, F32)],
        in_specs=[VMEM, each((BIN, ROWS)), each((BHID, ROWS)), each((BIN, BHID)), each((BHID, BIN))],
        out_specs=[pieces(1), columns(BIN // 2, BHID), columns(BIN // 2, BHID)],
        scratch_shapes=[HELD],
        compiler_params=params(24),
        cost_estimate=cost(1800, 11),
    )(msg, stay(saved), stay(slope), stay(left), stay(down))


def out(place, msg, left, cot):
    half = (BIN // 2, OWNED * BIN)
    return pl.pallas_call(
        out_kernel,
        out_shape=[far((ROWS, OWNED * BIN), BF16), shape(half, BF16), shape(half, F32)],
        in_specs=[SMEM, VMEM, ANY, ANY],
        out_specs=[ANY, VMEM, VMEM],
        scratch_shapes=[HELD, SQUARES, FLAT, FLAT, ONE, ONE, SEMS],
        compiler_params=params(20),
        cost_estimate=cost(3000, 16),
    )(place, msg, stay(left), stay(cot))


def into(msg, rightw):
    return pl.pallas_call(
        in_kernel,
        out_shape=far((ROWS, OWNED * BIN), BF16),
        in_specs=[VMEM, ANY],
        out_specs=ANY,
        scratch_shapes=[HELD, SQUARES, FLAT, ONE, SEMS],
        compiler_params=params(20),
        cost_estimate=cost(300, 3),
    )(msg, stay(rightw))


def exchange(msg):
    return lax.all_to_all(msg, "blk", split_axis=0, concat_axis=0, tiled=True)


def join_kernel(up_keep_ref, up_far_ref, down_keep_ref, down_far_ref, out_ref):
    at = 0
    for kept, far_ref in ((up_keep_ref, up_far_ref), (down_keep_ref, down_far_ref)):
        cols = slice(at, at + kept.shape[1])
        at += kept.shape[1]
        total = (kept[...] + far_ref[...].astype(F32)).astype(BF16)
        for n in range(out_ref.shape[0]):
            out_ref[n, :, cols] = total[2 * n : 2 * n + 2]


def join(up_keep, up_far, down_keep, down_far):
    dims = (up_keep.shape[0] // 2, 2, up_keep.shape[1] + down_keep.shape[1])
    return pl.pallas_call(
        join_kernel,
        out_shape=shape(dims, BF16),
        in_specs=[VMEM] * 4,
        out_specs=VMEM,
        compiler_params=params(8),
        cost_estimate=cost(1, 1),
    )(up_keep, up_far, down_keep, down_far)


def axis_of(bit):
    return DP[len(DP) - 1 - bit]


def swap_halves(send, bit):
    return lax.ppermute(send, axis_of(bit), [(0, 1), (1, 0)])


def halve(send, keep, bit):
    total = keep + swap_halves(send, bit).astype(F32)
    rows = total.shape[0] // 2
    return total[:rows].astype(BF16), total[rows:]


def finish_kernel(factor, in_ref, up_ref, down_ref):
    total = in_ref[0].astype(F32)
    for n in range(1, in_ref.shape[0]):
        total = total + in_ref[n].astype(F32)
    total = total * factor
    at = 0
    for ref in (up_ref, down_ref):
        for k in range(OWNED):
            ref[k] = total[:, at : at + ref.shape[2]]
            at += ref.shape[2]


def finish(pieces_in, factor):
    rows = pieces_in.shape[1]
    return pl.pallas_call(
        functools.partial(finish_kernel, factor),
        out_shape=[shape((OWNED, rows, BHID), F32), shape((OWNED, rows, BIN), F32)],
        in_specs=[VMEM],
        out_specs=[VMEM] * 2,
        compiler_params=params(8),
        cost_estimate=cost(1, 1),
    )(pieces_in)


def sum_over_dp(up_half, down_half, grad_u, factor):
    for bit in UP_STEPS[:-1]:
        up_half = halve(*up_half, bit)
    for bit in DOWN_STEPS[:-1]:
        down_half = halve(*down_half, bit)
    up_send, up_keep = up_half
    down_send, down_keep = down_half
    up_far, down_far = swap_halves(up_send, UP_STEPS[-1]), swap_halves(down_send, DOWN_STEPS[-1])
    total = join(up_keep, up_far, down_keep, down_far)
    total, grad_u = lax.optimization_barrier((total, grad_u))
    total = lax.all_to_all(total, tuple(axis_of(bit) for bit in SHARED), 0, 0, tiled=True)
    return (*finish(total, factor), grad_u)


def on_device(tokens, up_right, up_left, down_right, down_left, cotangent):
    place = lax.axis_index(DP).reshape(1).astype(jnp.int32)
    factor = 1.0 / math.sqrt(tokens.shape[0] * lax.axis_size(DP))
    v = exchange(right(tokens, up_right, TT))
    grad_z = exchange(right(cotangent, down_left, NT))
    z, saved, slope = up(place, v, up_left, down_right)
    w = exchange(z)
    grad_v, up_send, up_keep = back(grad_z, saved, slope, up_left, down_right)
    grad_u = exchange(grad_v)
    layer_out, down_send, down_keep = out(place, w, down_left, cotangent)
    up_grad, down_grad, grad_u = sum_over_dp((up_send, up_keep), (down_send, down_keep), grad_u, factor)
    input_grad = into(grad_u, up_right)
    return (layer_out, input_grad, up_grad, down_grad)


def solution(mesh):
    fine = jax.sharding.Mesh(mesh.devices.reshape((2,) * len(DP) + (GROUPS,)), DP + ("blk",))
    placed = (
        P(DP, "blk"),
        P("blk", None, None),
        P("blk", None, None),
        P("blk", None, None),
        P("blk", None, None),
        P(DP, "blk"),
    )
    return jax.shard_map(
        on_device,
        mesh=fine,
        in_specs=placed,
        out_specs=(P(DP, "blk"), P(DP, "blk"), P("blk", DP, None), P("blk", DP, None)),
        check_vma=False,
    )
```

```python
import functools
import math

import jax
import jax.numpy as jnp
from jax import lax
from jax.experimental import pallas as pl
from jax.experimental.pallas import tpu as pltpu
from jax.sharding import PartitionSpec as P

GROUPS = 8
OWNED = 8
BIN = 128
BHID = 512
ROWS = 512
PIECE = 16
PAIR = 2
UP_STEPS = (2, 0)
DOWN_STEPS = (0, 2)
SHARED = (5, 4, 3, 1)
DP = ("z8", "z4", "z2", "z1", "far", "core")
MIB = 1 << 20
BF16 = jnp.bfloat16
F32 = jnp.float32

NN = (((1,), (0,)), ((), ()))
NT = (((1,), (1,)), ((), ()))
TN = (((0,), (0,)), ((), ()))
TT = (((0,), (1,)), ((), ()))


def dot(a, b, dims):
    return lax.dot_general(a, b, dims, preferred_element_type=F32)


def swap_matrix():
    to = lax.broadcasted_iota(jnp.int32, (BIN, BIN), 0)
    come = lax.broadcasted_iota(jnp.int32, (BIN, BIN), 1)
    wanted = ((to & 14) << 3) | ((to >> 4) << 1) | (to & 1)
    return jnp.where(come == wanted, 1.0, 0.0).astype(BF16)


def shard_matrix(steps, place):
    to = lax.broadcasted_iota(jnp.int32, (BIN, BIN), 0)
    come = lax.broadcasted_iota(jnp.int32, (BIN, BIN), 1)
    owner = jnp.zeros_like(to)
    for at, bit in enumerate(steps + SHARED):
        here = (to >> (len(steps + SHARED) - at)) & 1
        if bit in steps:
            here = (1 - here) ^ ((place >> bit) & 1)
        owner = owner | (here << bit)
    return jnp.where(come == ((owner << 1) | (to & 1)), 1.0, 0.0).astype(BF16)


def scatter_rows(out_ref, slot, value):
    for n in range(GROUPS):
        out_ref[n, slot * PIECE : (slot + 1) * PIECE, :] = value[n * PIECE : (n + 1) * PIECE, :]


def gather_rows(msg_ref, held_ref):
    swap = swap_matrix()
    for src in range(GROUPS):
        swapped = dot(swap, msg_ref[src], NN).astype(BF16)
        for b in range(OWNED):
            held_ref[b, src * PIECE : (src + 1) * PIECE, :] = swapped[b * PIECE : (b + 1) * PIECE, :]


def fetch(src, dst, sem):
    copy = pltpu.make_async_copy(src, dst, sem)
    copy.start()
    return copy


def right_kernel(dims, x_hbm, w_hbm, out_hbm, x_ref, w_ref, out_ref, w_sem, in_sem, out_sem):
    w_copy = fetch(w_hbm, w_ref, w_sem)
    wide = PAIR * BIN
    x_copies = []
    for p in range(OWNED // PAIR):
        cols = pl.ds(p * wide, wide)
        x_copies.append(fetch(x_hbm.at[:, cols], x_ref.at[:, cols], in_sem.at[p]))
    w_copy.wait()
    out_copies = []
    for p in range(OWNED // PAIR):
        x_copies[p].wait()
        for k in range(p * PAIR, (p + 1) * PAIR):
            value = dot(w_ref[k], x_ref[:, k * BIN : (k + 1) * BIN], dims).astype(BF16)
            scatter_rows(out_ref, k, value)
        rows = pl.ds(p * PAIR * PIECE, PAIR * PIECE)
        out_copies.append(fetch(out_ref.at[:, rows, :], out_hbm.at[:, rows, :], out_sem.at[p]))
    for copy in out_copies:
        copy.wait()


def up_kernel(place_ref, msg_ref, left_ref, down_ref, out_ref, saved_ref, slope_ref, held_ref, shard_ref):
    j = pl.program_id(0)

    @pl.when(j == 0)
    def _():
        gather_rows(msg_ref, held_ref)
        shard_ref[...] = shard_matrix(UP_STEPS, place_ref[0])

    v = held_ref[j]
    saved_ref[0] = dot(shard_ref[...], v, NN).astype(BF16)
    s = dot(left_ref[0], v, TN)
    c = math.sqrt(2.0 / math.pi)
    square = s * s
    th = jnp.tanh(s * (c + (c * 0.044715) * square))
    half = 0.5 + 0.5 * th
    hidden = (s * half).astype(BF16)
    slope = half + (0.5 * s) * ((1.0 - th * th) * (c + (3.0 * c * 0.044715) * square))
    slope_ref[0] = slope.astype(BF16)
    z = dot(down_ref[0], hidden, TN).astype(BF16)
    scatter_rows(out_ref, 0, z)


def back_kernel(msg_ref, saved_ref, slope_ref, left_ref, down_ref, out_ref, send_ref, keep_ref, held_ref):
    j = pl.program_id(0)

    @pl.when(j == 0)
    def _():
        gather_rows(msg_ref, held_ref)

    grad_hidden = dot(down_ref[0], held_ref[j], NN)
    grad_pre = (grad_hidden * slope_ref[0].astype(F32)).astype(BF16)
    grad_v = dot(left_ref[0], grad_pre, NN).astype(BF16)
    scatter_rows(out_ref, 0, grad_v)
    part = dot(saved_ref[0], grad_pre, NT)
    send_ref[...] = part[: BIN // 2].astype(BF16)
    keep_ref[...] = part[BIN // 2 :]


def down_kernel(place_ref, msg_ref, cot_hbm, send_ref, keep_ref, held_ref, cot_ref, in_sem):
    cot_copy = fetch(cot_hbm, cot_ref, in_sem)
    shard = shard_matrix(DOWN_STEPS, place_ref[0])
    gather_rows(msg_ref, held_ref)
    cot_copy.wait()
    for k in range(OWNED):
        cols = slice(k * BIN, (k + 1) * BIN)
        part = dot(dot(shard, held_ref[k], NN).astype(BF16), cot_ref[:, cols], NN)
        send_ref[:, cols] = part[: BIN // 2].astype(BF16)
        keep_ref[:, cols] = part[BIN // 2 :]


def out_kernel(msg_ref, left_hbm, out_hbm, held_ref, left_ref, out_ref, left_sem, out_sem):
    wide = PAIR * BIN
    left_copy = fetch(left_hbm, left_ref, left_sem)
    gather_rows(msg_ref, held_ref)
    left_copy.wait()
    out_copies = []
    for p in range(OWNED // PAIR):
        for k in range(p * PAIR, (p + 1) * PAIR):
            out_ref[:, k * BIN : (k + 1) * BIN] = dot(held_ref[k], left_ref[k], TN).astype(BF16)
        cols = pl.ds(p * wide, wide)
        out_copies.append(fetch(out_ref.at[:, cols], out_hbm.at[:, cols], out_sem.at[p]))
    for copy in out_copies:
        copy.wait()


def in_kernel(msg_ref, right_hbm, out_hbm, held_ref, right_ref, out_ref, right_sem, out_sem):
    wide = PAIR * BIN
    right_copy = fetch(right_hbm, right_ref, right_sem)
    gather_rows(msg_ref, held_ref)
    right_copy.wait()
    out_copies = []
    for p in range(OWNED // PAIR):
        for k in range(p * PAIR, (p + 1) * PAIR):
            out_ref[:, k * BIN : (k + 1) * BIN] = dot(held_ref[k], right_ref[k], TT).astype(BF16)
        cols = pl.ds(p * wide, wide)
        out_copies.append(fetch(out_ref.at[:, cols], out_hbm.at[:, cols], out_sem.at[p]))
    for copy in out_copies:
        copy.wait()


VMEM = pl.BlockSpec(memory_space=pltpu.VMEM)
SMEM = pl.BlockSpec(memory_space=pltpu.SMEM)
MSG = (GROUPS, BIN, ROWS)


def params(mib):
    return pltpu.CompilerParams(vmem_limit_bytes=mib * MIB)


def cost(mflop, mib, trans=0):
    return pl.CostEstimate(flops=mflop * 1000000, bytes_accessed=mib * MIB, transcendentals=trans)


def shape(dims, dtype):
    return jax.ShapeDtypeStruct(dims, dtype)


def far(dims, dtype):
    return pltpu.HBM(dims, dtype)


def stay(x):
    return pltpu.with_memory_space_constraint(x, pltpu.HBM)


def each(dims, count=1):
    return pl.BlockSpec((count,) + dims, lambda j: (j, 0, 0))


def pieces(count):
    return pl.BlockSpec((GROUPS, count * PIECE, ROWS), lambda j: (0, j, 0))


def columns(rows, width):
    return pl.BlockSpec((rows, width), lambda j: (0, j))


HELD = pltpu.VMEM((OWNED, BIN, ROWS), BF16)
SHARD = pltpu.VMEM((BIN, BIN), BF16)


ANY = pl.BlockSpec(memory_space=pl.ANY)
SQUARES = pltpu.VMEM((OWNED, BIN, BIN), BF16)
FLAT = pltpu.VMEM((ROWS, OWNED * BIN), BF16)
ONE = pltpu.SemaphoreType.DMA
SEMS = pltpu.SemaphoreType.DMA((OWNED // PAIR,))


def right(x, w, dims):
    return pl.pallas_call(
        functools.partial(right_kernel, dims),
        out_shape=far(MSG, BF16),
        in_specs=[ANY, ANY],
        out_specs=ANY,
        scratch_shapes=[FLAT, SQUARES, pltpu.VMEM(MSG, BF16), ONE, SEMS, SEMS],
        compiler_params=params(16),
        cost_estimate=cost(134, 3),
    )(stay(x), stay(w))


def up(place, msg, left, down):
    return pl.pallas_call(
        up_kernel,
        grid=(OWNED,),
        out_shape=[far(MSG, BF16), far((OWNED, BIN, ROWS), BF16), far((OWNED, BHID, ROWS), BF16)],
        in_specs=[SMEM, VMEM, each((BIN, BHID)), each((BHID, BIN))],
        out_specs=[pieces(1), each((BIN, ROWS)), each((BHID, ROWS))],
        scratch_shapes=[HELD, SHARD],
        compiler_params=params(24),
        cost_estimate=cost(1300, 9, OWNED * BHID * ROWS),
    )(place, msg, stay(left), stay(down))


def back(msg, saved, slope, left, down):
    half = (BIN // 2, OWNED * BHID)
    return pl.pallas_call(
        back_kernel,
        grid=(OWNED,),
        out_shape=[far(MSG, BF16), far(half, BF16), far(half, F32)],
        in_specs=[VMEM, each((BIN, ROWS)), each((BHID, ROWS)), each((BIN, BHID)), each((BHID, BIN))],
        out_specs=[pieces(1), columns(BIN // 2, BHID), columns(BIN // 2, BHID)],
        scratch_shapes=[HELD],
        compiler_params=params(24),
        cost_estimate=cost(1800, 11),
    )(msg, stay(saved), stay(slope), stay(left), stay(down))


def down(place, msg, cot):
    half = (BIN // 2, OWNED * BIN)
    return pl.pallas_call(
        down_kernel,
        out_shape=[shape(half, BF16), shape(half, F32)],
        in_specs=[SMEM, VMEM, ANY],
        out_specs=[VMEM, VMEM],
        scratch_shapes=[HELD, FLAT, ONE],
        compiler_params=params(20),
        cost_estimate=cost(3000, 16),
    )(place, msg, stay(cot))


def out(msg, left):
    return pl.pallas_call(
        out_kernel,
        out_shape=far((ROWS, OWNED * BIN), BF16),
        in_specs=[VMEM, ANY],
        out_specs=ANY,
        scratch_shapes=[HELD, SQUARES, FLAT, ONE, SEMS],
        compiler_params=params(20),
        cost_estimate=cost(134, 3),
    )(msg, stay(left))


def into(msg, rightw):
    return pl.pallas_call(
        in_kernel,
        out_shape=far((ROWS, OWNED * BIN), BF16),
        in_specs=[VMEM, ANY],
        out_specs=ANY,
        scratch_shapes=[HELD, SQUARES, FLAT, ONE, SEMS],
        compiler_params=params(20),
        cost_estimate=cost(300, 3),
    )(msg, stay(rightw))


def exchange(msg):
    return lax.all_to_all(msg, "blk", split_axis=0, concat_axis=0, tiled=True)


def join_kernel(up_keep_ref, up_far_ref, down_keep_ref, down_far_ref, out_ref):
    at = 0
    for kept, far_ref in ((up_keep_ref, up_far_ref), (down_keep_ref, down_far_ref)):
        cols = slice(at, at + kept.shape[1])
        at += kept.shape[1]
        total = (kept[...] + far_ref[...].astype(F32)).astype(BF16)
        for n in range(out_ref.shape[0]):
            out_ref[n, :, cols] = total[2 * n : 2 * n + 2]


def join(up_keep, up_far, down_keep, down_far):
    dims = (up_keep.shape[0] // 2, 2, up_keep.shape[1] + down_keep.shape[1])
    return pl.pallas_call(
        join_kernel,
        out_shape=shape(dims, BF16),
        in_specs=[VMEM] * 4,
        out_specs=VMEM,
        compiler_params=params(8),
        cost_estimate=cost(1, 1),
    )(up_keep, up_far, down_keep, down_far)


def axis_of(bit):
    return DP[len(DP) - 1 - bit]


def swap_halves(send, bit):
    return lax.ppermute(send, axis_of(bit), [(0, 1), (1, 0)])


def halve(send, keep, bit):
    total = keep + swap_halves(send, bit).astype(F32)
    rows = total.shape[0] // 2
    return total[:rows].astype(BF16), total[rows:]


def finish_kernel(factor, in_ref, up_ref, down_ref):
    total = in_ref[0].astype(F32)
    for n in range(1, in_ref.shape[0]):
        total = total + in_ref[n].astype(F32)
    total = total * factor
    at = 0
    for ref in (up_ref, down_ref):
        for k in range(OWNED):
            ref[k] = total[:, at : at + ref.shape[2]]
            at += ref.shape[2]


def finish(pieces_in, factor):
    rows = pieces_in.shape[1]
    return pl.pallas_call(
        functools.partial(finish_kernel, factor),
        out_shape=[shape((OWNED, rows, BHID), F32), shape((OWNED, rows, BIN), F32)],
        in_specs=[VMEM],
        out_specs=[VMEM] * 2,
        compiler_params=params(8),
        cost_estimate=cost(1, 1),
    )(pieces_in)


def sum_over_dp(up_half, down_half, grad_u, layer_out, factor):
    for bit in UP_STEPS[:-1]:
        up_half = halve(*up_half, bit)
    for bit in DOWN_STEPS[:-1]:
        down_half = halve(*down_half, bit)
    up_send, up_keep = up_half
    down_send, down_keep = down_half
    up_far, down_far = swap_halves(up_send, UP_STEPS[-1]), swap_halves(down_send, DOWN_STEPS[-1])
    total = join(up_keep, up_far, down_keep, down_far)
    total, grad_u, layer_out = lax.optimization_barrier((total, grad_u, layer_out))
    total = lax.all_to_all(total, tuple(axis_of(bit) for bit in SHARED), 0, 0, tiled=True)
    return (*finish(total, factor), grad_u, layer_out)


def on_device(tokens, up_right, up_left, down_right, down_left, cotangent):
    place = lax.axis_index(DP).reshape(1).astype(jnp.int32)
    factor = 1.0 / math.sqrt(tokens.shape[0] * lax.axis_size(DP))
    v = exchange(right(tokens, up_right, TT))
    grad_z = exchange(right(cotangent, down_left, NT))
    z, saved, slope = up(place, v, up_left, down_right)
    w = exchange(z)
    grad_v, up_send, up_keep = back(grad_z, saved, slope, up_left, down_right)
    grad_u = exchange(grad_v)
    down_half = down(place, w, cotangent)
    layer_out = out(w, down_left)
    up_grad, down_grad, grad_u, layer_out = sum_over_dp(
        (up_send, up_keep), down_half, grad_u, layer_out, factor
    )
    input_grad = into(grad_u, up_right)
    return (layer_out, input_grad, up_grad, down_grad)


def solution(mesh):
    fine = jax.sharding.Mesh(mesh.devices.reshape((2,) * len(DP) + (GROUPS,)), DP + ("blk",))
    placed = (
        P(DP, "blk"),
        P("blk", None, None),
        P("blk", None, None),
        P("blk", None, None),
        P("blk", None, None),
        P(DP, "blk"),
    )
    return jax.shard_map(
        on_device,
        mesh=fine,
        in_specs=placed,
        out_specs=(P(DP, "blk"), P(DP, "blk"), P("blk", DP, None), P("blk", DP, None)),
        check_vma=False,
    )
```

```python
import functools
import math

import jax
import jax.numpy as jnp
from jax import lax
from jax.experimental import pallas as pl
from jax.experimental.pallas import tpu as pltpu
from jax.sharding import PartitionSpec as P

GROUPS = 8
OWNED = 8
BIN = 128
BHID = 512
ROWS = 512
PIECE = 16
PAIR = 2
UP_STEPS = (2, 0)
DOWN_STEPS = (2, 0)
SHARED = (5, 4, 3, 1)
DP = ("z8", "z4", "z2", "z1", "far", "core")
MIB = 1 << 20
BF16 = jnp.bfloat16
F32 = jnp.float32

NN = (((1,), (0,)), ((), ()))
NT = (((1,), (1,)), ((), ()))
TN = (((0,), (0,)), ((), ()))
TT = (((0,), (1,)), ((), ()))


def dot(a, b, dims):
    return lax.dot_general(a, b, dims, preferred_element_type=F32)


def swap_matrix():
    to = lax.broadcasted_iota(jnp.int32, (BIN, BIN), 0)
    come = lax.broadcasted_iota(jnp.int32, (BIN, BIN), 1)
    wanted = ((to & 14) << 3) | ((to >> 4) << 1) | (to & 1)
    return jnp.where(come == wanted, 1.0, 0.0).astype(BF16)


def shard_matrix(steps, place):
    to = lax.broadcasted_iota(jnp.int32, (BIN, BIN), 0)
    come = lax.broadcasted_iota(jnp.int32, (BIN, BIN), 1)
    owner = jnp.zeros_like(to)
    for at, bit in enumerate(steps + SHARED):
        here = (to >> (len(steps + SHARED) - at)) & 1
        if bit in steps:
            here = (1 - here) ^ ((place >> bit) & 1)
        owner = owner | (here << bit)
    return jnp.where(come == ((owner << 1) | (to & 1)), 1.0, 0.0).astype(BF16)


def scatter_rows(out_ref, slot, value):
    for n in range(GROUPS):
        out_ref[n, slot * PIECE : (slot + 1) * PIECE, :] = value[n * PIECE : (n + 1) * PIECE, :]


def gather_rows(msg_ref, held_ref):
    swap = swap_matrix()
    for src in range(GROUPS):
        swapped = dot(swap, msg_ref[src], NN).astype(BF16)
        for b in range(OWNED):
            held_ref[b, src * PIECE : (src + 1) * PIECE, :] = swapped[b * PIECE : (b + 1) * PIECE, :]


def fetch(src, dst, sem):
    copy = pltpu.make_async_copy(src, dst, sem)
    copy.start()
    return copy


def right_kernel(dims, x_hbm, w_hbm, out_hbm, x_ref, w_ref, out_ref, w_sem, in_sem, out_sem):
    w_copy = fetch(w_hbm, w_ref, w_sem)
    wide = PAIR * BIN
    x_copies = []
    for p in range(OWNED // PAIR):
        cols = pl.ds(p * wide, wide)
        x_copies.append(fetch(x_hbm.at[:, cols], x_ref.at[:, cols], in_sem.at[p]))
    w_copy.wait()
    out_copies = []
    for p in range(OWNED // PAIR):
        x_copies[p].wait()
        for k in range(p * PAIR, (p + 1) * PAIR):
            value = dot(w_ref[k], x_ref[:, k * BIN : (k + 1) * BIN], dims).astype(BF16)
            scatter_rows(out_ref, k, value)
        rows = pl.ds(p * PAIR * PIECE, PAIR * PIECE)
        out_copies.append(fetch(out_ref.at[:, rows, :], out_hbm.at[:, rows, :], out_sem.at[p]))
    for copy in out_copies:
        copy.wait()


def up_kernel(place_ref, msg_ref, left_ref, down_ref, out_ref, saved_ref, slope_ref, held_ref, shard_ref):
    j = pl.program_id(0)

    @pl.when(j == 0)
    def _():
        gather_rows(msg_ref, held_ref)
        shard_ref[...] = shard_matrix(UP_STEPS, place_ref[0])

    v = held_ref[j]
    saved_ref[0] = dot(shard_ref[...], v, NN).astype(BF16)
    s = dot(left_ref[0], v, TN)
    c = math.sqrt(2.0 / math.pi)
    square = s * s
    th = jnp.tanh(s * (c + (c * 0.044715) * square))
    half = 0.5 + 0.5 * th
    hidden = (s * half).astype(BF16)
    slope = half + (0.5 * s) * ((1.0 - th * th) * (c + (3.0 * c * 0.044715) * square))
    slope_ref[0] = slope.astype(BF16)
    z = dot(down_ref[0], hidden, TN).astype(BF16)
    scatter_rows(out_ref, 0, z)


def back_kernel(msg_ref, saved_ref, slope_ref, left_ref, down_ref, out_ref, send_ref, keep_ref, held_ref):
    j = pl.program_id(0)

    @pl.when(j == 0)
    def _():
        gather_rows(msg_ref, held_ref)

    grad_hidden = dot(down_ref[0], held_ref[j], NN)
    grad_pre = (grad_hidden * slope_ref[0].astype(F32)).astype(BF16)
    grad_v = dot(left_ref[0], grad_pre, NN).astype(BF16)
    scatter_rows(out_ref, 0, grad_v)
    part = dot(saved_ref[0], grad_pre, NT)
    send_ref[...] = part[: BIN // 2].astype(BF16)
    keep_ref[...] = part[BIN // 2 :]


def down_kernel(place_ref, msg_ref, cot_hbm, send_ref, keep_ref, held_ref, cot_ref, in_sem):
    cot_copy = fetch(cot_hbm, cot_ref, in_sem)
    shard = shard_matrix(DOWN_STEPS, place_ref[0])
    gather_rows(msg_ref, held_ref)
    cot_copy.wait()
    for k in range(OWNED):
        cols = slice(k * BIN, (k + 1) * BIN)
        part = dot(dot(shard, held_ref[k], NN).astype(BF16), cot_ref[:, cols], NN)
        send_ref[:, cols] = part[: BIN // 2].astype(BF16)
        keep_ref[:, cols] = part[BIN // 2 :]


def out_kernel(msg_ref, left_hbm, out_hbm, held_ref, left_ref, out_ref, left_sem, out_sem):
    wide = PAIR * BIN
    left_copy = fetch(left_hbm, left_ref, left_sem)
    gather_rows(msg_ref, held_ref)
    left_copy.wait()
    out_copies = []
    for p in range(OWNED // PAIR):
        for k in range(p * PAIR, (p + 1) * PAIR):
            out_ref[:, k * BIN : (k + 1) * BIN] = dot(held_ref[k], left_ref[k], TN).astype(BF16)
        cols = pl.ds(p * wide, wide)
        out_copies.append(fetch(out_ref.at[:, cols], out_hbm.at[:, cols], out_sem.at[p]))
    for copy in out_copies:
        copy.wait()


def in_kernel(msg_ref, right_hbm, out_hbm, held_ref, right_ref, out_ref, right_sem, out_sem):
    wide = PAIR * BIN
    right_copy = fetch(right_hbm, right_ref, right_sem)
    gather_rows(msg_ref, held_ref)
    right_copy.wait()
    out_copies = []
    for p in range(OWNED // PAIR):
        for k in range(p * PAIR, (p + 1) * PAIR):
            out_ref[:, k * BIN : (k + 1) * BIN] = dot(held_ref[k], right_ref[k], TT).astype(BF16)
        cols = pl.ds(p * wide, wide)
        out_copies.append(fetch(out_ref.at[:, cols], out_hbm.at[:, cols], out_sem.at[p]))
    for copy in out_copies:
        copy.wait()


VMEM = pl.BlockSpec(memory_space=pltpu.VMEM)
SMEM = pl.BlockSpec(memory_space=pltpu.SMEM)
MSG = (GROUPS, BIN, ROWS)


def params(mib):
    return pltpu.CompilerParams(vmem_limit_bytes=mib * MIB)


def cost(mflop, mib, trans=0):
    return pl.CostEstimate(flops=mflop * 1000000, bytes_accessed=mib * MIB, transcendentals=trans)


def shape(dims, dtype):
    return jax.ShapeDtypeStruct(dims, dtype)


def far(dims, dtype):
    return pltpu.HBM(dims, dtype)


def stay(x):
    return pltpu.with_memory_space_constraint(x, pltpu.HBM)


def each(dims, count=1):
    return pl.BlockSpec((count,) + dims, lambda j: (j, 0, 0))


def pieces(count):
    return pl.BlockSpec((GROUPS, count * PIECE, ROWS), lambda j: (0, j, 0))


def columns(rows, width):
    return pl.BlockSpec((rows, width), lambda j: (0, j))


HELD = pltpu.VMEM((OWNED, BIN, ROWS), BF16)
SHARD = pltpu.VMEM((BIN, BIN), BF16)


ANY = pl.BlockSpec(memory_space=pl.ANY)
SQUARES = pltpu.VMEM((OWNED, BIN, BIN), BF16)
FLAT = pltpu.VMEM((ROWS, OWNED * BIN), BF16)
ONE = pltpu.SemaphoreType.DMA
SEMS = pltpu.SemaphoreType.DMA((OWNED // PAIR,))


def right(x, w, dims):
    return pl.pallas_call(
        functools.partial(right_kernel, dims),
        out_shape=far(MSG, BF16),
        in_specs=[ANY, ANY],
        out_specs=ANY,
        scratch_shapes=[FLAT, SQUARES, pltpu.VMEM(MSG, BF16), ONE, SEMS, SEMS],
        compiler_params=params(16),
        cost_estimate=cost(134, 3),
    )(stay(x), stay(w))


def up(place, msg, left, down):
    return pl.pallas_call(
        up_kernel,
        grid=(OWNED,),
        out_shape=[far(MSG, BF16), far((OWNED, BIN, ROWS), BF16), far((OWNED, BHID, ROWS), BF16)],
        in_specs=[SMEM, VMEM, each((BIN, BHID)), each((BHID, BIN))],
        out_specs=[pieces(1), each((BIN, ROWS)), each((BHID, ROWS))],
        scratch_shapes=[HELD, SHARD],
        compiler_params=params(24),
        cost_estimate=cost(1300, 9, OWNED * BHID * ROWS),
    )(place, msg, stay(left), stay(down))


def back(msg, saved, slope, left, down):
    half = (BIN // 2, OWNED * BHID)
    return pl.pallas_call(
        back_kernel,
        grid=(OWNED,),
        out_shape=[far(MSG, BF16), far(half, BF16), far(half, F32)],
        in_specs=[VMEM, each((BIN, ROWS)), each((BHID, ROWS)), each((BIN, BHID)), each((BHID, BIN))],
        out_specs=[pieces(1), columns(BIN // 2, BHID), columns(BIN // 2, BHID)],
        scratch_shapes=[HELD],
        compiler_params=params(24),
        cost_estimate=cost(1800, 11),
    )(msg, stay(saved), stay(slope), stay(left), stay(down))


def down(place, msg, cot):
    half = (BIN // 2, OWNED * BIN)
    return pl.pallas_call(
        down_kernel,
        out_shape=[shape(half, BF16), shape(half, F32)],
        in_specs=[SMEM, VMEM, ANY],
        out_specs=[VMEM, VMEM],
        scratch_shapes=[HELD, FLAT, ONE],
        compiler_params=params(20),
        cost_estimate=cost(3000, 16),
    )(place, msg, stay(cot))


def out(msg, left):
    return pl.pallas_call(
        out_kernel,
        out_shape=far((ROWS, OWNED * BIN), BF16),
        in_specs=[VMEM, ANY],
        out_specs=ANY,
        scratch_shapes=[HELD, SQUARES, FLAT, ONE, SEMS],
        compiler_params=params(20),
        cost_estimate=cost(134, 3),
    )(msg, stay(left))


def into(msg, rightw):
    return pl.pallas_call(
        in_kernel,
        out_shape=far((ROWS, OWNED * BIN), BF16),
        in_specs=[VMEM, ANY],
        out_specs=ANY,
        scratch_shapes=[HELD, SQUARES, FLAT, ONE, SEMS],
        compiler_params=params(20),
        cost_estimate=cost(300, 3),
    )(msg, stay(rightw))


def exchange(msg):
    return lax.all_to_all(msg, "blk", split_axis=0, concat_axis=0, tiled=True)


def join_kernel(up_keep_ref, up_far_ref, down_keep_ref, down_far_ref, out_ref):
    at = 0
    for kept, far_ref in ((up_keep_ref, up_far_ref), (down_keep_ref, down_far_ref)):
        cols = slice(at, at + kept.shape[1])
        at += kept.shape[1]
        total = (kept[...] + far_ref[...].astype(F32)).astype(BF16)
        for n in range(out_ref.shape[0]):
            out_ref[n, :, cols] = total[2 * n : 2 * n + 2]


def join(up_keep, up_far, down_keep, down_far):
    dims = (up_keep.shape[0] // 2, 2, up_keep.shape[1] + down_keep.shape[1])
    return pl.pallas_call(
        join_kernel,
        out_shape=shape(dims, BF16),
        in_specs=[VMEM] * 4,
        out_specs=VMEM,
        compiler_params=params(8),
        cost_estimate=cost(1, 1),
    )(up_keep, up_far, down_keep, down_far)


def axis_of(bit):
    return DP[len(DP) - 1 - bit]


def swap_halves(send, bit):
    return lax.ppermute(send, axis_of(bit), [(0, 1), (1, 0)])


def halve(send, keep, bit):
    total = keep + swap_halves(send, bit).astype(F32)
    rows = total.shape[0] // 2
    return total[:rows].astype(BF16), total[rows:]


def finish_kernel(factor, in_ref, up_ref, down_ref):
    total = in_ref[0].astype(F32)
    for n in range(1, in_ref.shape[0]):
        total = total + in_ref[n].astype(F32)
    total = total * factor
    at = 0
    for ref in (up_ref, down_ref):
        for k in range(OWNED):
            ref[k] = total[:, at : at + ref.shape[2]]
            at += ref.shape[2]


def finish(pieces_in, factor):
    rows = pieces_in.shape[1]
    return pl.pallas_call(
        functools.partial(finish_kernel, factor),
        out_shape=[shape((OWNED, rows, BHID), F32), shape((OWNED, rows, BIN), F32)],
        in_specs=[VMEM],
        out_specs=[VMEM] * 2,
        compiler_params=params(8),
        cost_estimate=cost(1, 1),
    )(pieces_in)


def sum_over_dp(up_half, down_half, grad_u, layer_out, factor):
    for bit in UP_STEPS[:-1]:
        up_half = halve(*up_half, bit)
    for bit in DOWN_STEPS[:-1]:
        down_half = halve(*down_half, bit)
    up_send, up_keep = up_half
    down_send, down_keep = down_half
    up_far, down_far = swap_halves(up_send, UP_STEPS[-1]), swap_halves(down_send, DOWN_STEPS[-1])
    total = join(up_keep, up_far, down_keep, down_far)
    total, grad_u, layer_out = lax.optimization_barrier((total, grad_u, layer_out))
    total = lax.all_to_all(total, tuple(axis_of(bit) for bit in SHARED), 0, 0, tiled=True)
    return (*finish(total, factor), grad_u, layer_out)


def on_device(tokens, up_right, up_left, down_right, down_left, cotangent):
    place = lax.axis_index(DP).reshape(1).astype(jnp.int32)
    factor = 1.0 / math.sqrt(tokens.shape[0] * lax.axis_size(DP))
    v = exchange(right(tokens, up_right, TT))
    grad_z = exchange(right(cotangent, down_left, NT))
    z, saved, slope = up(place, v, up_left, down_right)
    w = exchange(z)
    grad_v, up_send, up_keep = back(grad_z, saved, slope, up_left, down_right)
    grad_u = exchange(grad_v)
    down_half = down(place, w, cotangent)
    layer_out = out(w, down_left)
    up_grad, down_grad, grad_u, layer_out = sum_over_dp(
        (up_send, up_keep), down_half, grad_u, layer_out, factor
    )
    input_grad = into(grad_u, up_right)
    return (layer_out, input_grad, up_grad, down_grad)


def solution(mesh):
    fine = jax.sharding.Mesh(mesh.devices.reshape((2,) * len(DP) + (GROUPS,)), DP + ("blk",))
    placed = (
        P(DP, "blk"),
        P("blk", None, None),
        P("blk", None, None),
        P("blk", None, None),
        P("blk", None, None),
        P(DP, "blk"),
    )
    return jax.shard_map(
        on_device,
        mesh=fine,
        in_specs=placed,
        out_specs=(P(DP, "blk"), P(DP, "blk"), P("blk", DP, None), P("blk", DP, None)),
        check_vma=False,
    )
```
